32 devices in a mesh: slab: 4 (over y, x), brick: 8 (over z, core).
Axes of the slice: x: 2, y: 2, z: 4, core: 2. Of those that a mesh axis runs over, the one named last changes fastest.
Arguments:
- occupancy: int32 [16, 64, 512], P('slab', 'brick'), may hold values 0 or 1
- modulus: float32 [16, 64, 512], P('slab', 'brick'), may hold values from 0.5 to 4
- displacement_start: float32 [2, 3, 16, 64, 512], P(None, None, 'slab', 'brick'), may hold values from -12 to 12
- direction_start: float32 [2, 3, 16, 64, 512], P(None, None, 'slab', 'brick'), may hold values from -12 to 12
- muscle_force: float32 [2, 40], replicated, may hold values from 16 to 512
- muscle_direction: float32 [2, 40, 3], replicated, may hold values from -4 to 4
- attachment_nodes: int32 [40, 128, 3], replicated, may hold values from 0 to 511, as said below
Outputs:
- displacement: float32 [2, 3, 16, 64, 512], P(None, None, 'slab', 'brick')
- sensitivity: float32 [2, 40], replicated
The draws below stay inside these ranges and needn't reach their ends.
Inputs may be any that keep to these rules, and one draw needn't show every extreme that they name: attachment_nodes[m, k] holds an x index below 16, a y index below 64 and a z index below 512; the nodes of one muscle lie within 4 indices of a centre along each dimension, and may repeat.
All inputs are finite; a program needn't handle non-finite values. No bound on the sum of `occupancy` on one device may be relied on, other than what follows from the above.
Results may differ from the reference program's by a relative error of at most 0.00028.
Values sent between devices are 32-bit elements; how exact they have to be, the bound alone decides.
A program may use at most 64 MiB of HBM per device.

```python
import math
import jax
import jax.numpy as jnp
import numpy as np
from jax import lax

ITERS = 2
MUSCLES = 40
ATTACH = 128
FRAMES = 2
NX = 16
NY = 64
NZ = 512


def spread_field(key, ramp):
    shape = (FRAMES, 3, NX, NY, NZ)
    noise = jax.random.truncated_normal(jax.random.fold_in(key, 2), -4.0, 4.0, shape, jnp.float32)
    values = ramp * noise
    return values.astype(jnp.float32)


def draw_displacement_start(key, part):
    along = (jnp.arange(NX, dtype=jnp.float32) + 0.5) / NX
    ramp = (3.0 - 2.0 * along).reshape(1, 1, NX, 1, 1)
    return spread_field(jax.random.fold_in(key, 21), ramp)


def draw_direction_start(key, part):
    across = (jnp.arange(NY, dtype=jnp.float32) + 0.5) / NY
    ramp = (1.0 + 2.0 * across).reshape(1, 1, 1, NY, 1)
    return spread_field(jax.random.fold_in(key, 22), ramp)


def draw_attachment_nodes(key, part):
    key_x = jax.random.fold_in(key, 11)
    key_y = jax.random.fold_in(key, 12)
    key_z = jax.random.fold_in(key, 13)
    key_offset = jax.random.fold_in(key, 14)
    centre_x = jax.random.randint(key_x, (MUSCLES, 1), 0, NX)
    centre_y = jax.random.randint(key_y, (MUSCLES, 1), 0, NY)
    centre_z = jax.random.randint(key_z, (MUSCLES, 1), 0, NZ)
    centre_x = centre_x.at[0, 0].set(NX - 1).at[1, 0].set(0)
    centre_y = centre_y.at[0, 0].set(NY - 1).at[1, 0].set(0)
    centre_z = centre_z.at[0, 0].set(NZ - 1).at[1, 0].set(0)
    offsets = jax.random.randint(key_offset, (MUSCLES, ATTACH, 3), -4, 5)
    offsets = offsets.at[0, 0].set(0).at[1, 0].set(0)
    coord_x = jnp.clip(centre_x + offsets[:, :, 0], 0, NX - 1)
    coord_y = jnp.clip(centre_y + offsets[:, :, 1], 0, NY - 1)
    coord_z = jnp.clip(centre_z + offsets[:, :, 2], 0, NZ - 1)
    return jnp.stack([coord_x, coord_y, coord_z], axis=2).astype(jnp.int32)


def with_ends(drawn, key, least, largest):
    longest = drawn.shape.index(max(drawn.shape))
    spots = []
    for shift in (0, 1):
        where = [jax.random.randint(jax.random.fold_in(key, axis), (), 0, length) for axis, length in enumerate(drawn.shape)]
        where[longest] = (where[longest] + shift) % drawn.shape[longest]
        spots.append(tuple(where))
    return drawn.at[spots[0]].set(least).at[spots[1]].set(largest)


def shard_levels(own_key, shape, split, low, high):
    loudness = 1.0
    for dim, shards_of in split:
        steps = jax.random.uniform(jax.random.fold_in(jax.random.fold_in(own_key, 6), dim), (shards_of,), jnp.float32, low / len(split), high / len(split))
        loudness = loudness * jnp.repeat(jnp.exp(steps), shape[dim] // shards_of).reshape((-1,) + (1,) * (len(shape) - 1 - dim))
    return loudness


def bell_draw(rng, dims, deviation, most, kind=jnp.bfloat16):
    array = jax.random.normal(rng, dims, jnp.float32) * deviation
    return jnp.minimum(jnp.maximum(array, -most), most).astype(kind)


def setup_inputs(seed: int = 0) -> dict:
    key_list = jax.random.split(jax.random.key(seed), 8)
    occupancy = with_ends((jax.random.randint(key_list[0], (NX, NY, NZ), 0, 5) < 3).astype(jnp.int32), jax.random.fold_in(key_list[0], 1), 0, 1)
    modulus = jnp.clip(jnp.exp(math.log(4.0) - 2.0794415 * jax.random.uniform(key_list[1], (NX, NY, NZ), jnp.float32) ** shard_levels(key_list[1], (NX, NY, NZ), ((0, 4), (1, 8)), -0.2, 0.2)), 0.5, 4.0)
    displacement_start = draw_displacement_start(jax.random.fold_in(key_list[7], 71), 0)
    direction_start = draw_direction_start(jax.random.fold_in(key_list[7], 71), 0)
    muscle_force = jnp.clip(jnp.exp(jax.random.uniform(key_list[4], (FRAMES, MUSCLES), jnp.float32, math.log(16.0), math.log(512.0))), 16.0, 512.0)
    muscle_direction = bell_draw(key_list[5], (FRAMES, MUSCLES, 3), 1.0, 4.0, jnp.float32)
    attachment_nodes = draw_attachment_nodes(jax.random.fold_in(key_list[7], 71), 0)
    return dict(occupancy=occupancy, modulus=modulus, displacement_start=displacement_start, direction_start=direction_start, muscle_force=muscle_force, muscle_direction=muscle_direction, attachment_nodes=attachment_nodes)


ersatz_modulus = 0.02

def corner_offsets():
    return [(step_x, step_y, step_z) for step_x in (0, 1) for step_y in (0, 1) for step_z in (0, 1)]

def element_matrix():
    poisson = 0.3
    lame_first = poisson / ((1.0 + poisson) * (1.0 - 2.0 * poisson))
    shear_modulus = 0.5 / (1.0 + poisson)
    elastic = np.zeros((6, 6))
    elastic[:3, :3] = lame_first
    for position in range(3):
        elastic[position, position] += 2.0 * shear_modulus
        elastic[position + 3, position + 3] = shear_modulus
    points = [0.5 - 0.5 / math.sqrt(3.0), 0.5 + 0.5 / math.sqrt(3.0)]
    matrix = np.zeros((24, 24))
    for point_x in points:
        for point_y in points:
            for point_z in points:
                strain = np.zeros((6, 24))
                for corner, (step_x, step_y, step_z) in enumerate(corner_offsets()):
                    weight_x = point_x if step_x else 1.0 - point_x
                    weight_y = point_y if step_y else 1.0 - point_y
                    weight_z = point_z if step_z else 1.0 - point_z
                    sign_x = 1.0 if step_x else -1.0
                    sign_y = 1.0 if step_y else -1.0
                    sign_z = 1.0 if step_z else -1.0
                    grad_x = sign_x * weight_y * weight_z
                    grad_y = weight_x * sign_y * weight_z
                    grad_z = weight_x * weight_y * sign_z
                    column = 3 * corner
                    strain[0, column] = grad_x
                    strain[1, column + 1] = grad_y
                    strain[2, column + 2] = grad_z
                    strain[3, column] = grad_y
                    strain[3, column + 1] = grad_x
                    strain[4, column + 1] = grad_z
                    strain[4, column + 2] = grad_y
                    strain[5, column] = grad_z
                    strain[5, column + 2] = grad_x
                matrix += strain.T @ elastic @ strain / 8.0
    return matrix.astype(np.float32)

def apply_stiffness(nodal_values, stiffness_scale, blocked_stiffness):
    padded = jnp.pad(nodal_values, ((0, 0), (0, 0), (0, 1), (0, 1), (0, 1)))
    corners = corner_offsets()
    summed = jnp.zeros((FRAMES, 3, NX + 1, NY + 1, NZ + 1), jnp.float32)
    for out_corner, (out_x, out_y, out_z) in enumerate(corners):
        forces = jnp.zeros((FRAMES, 3, NX, NY, NZ), jnp.float32)
        for in_corner, (in_x, in_y, in_z) in enumerate(corners):
            corner_values = padded[:, :, in_x:in_x + NX, in_y:in_y + NY, in_z:in_z + NZ]
            forces = forces + jnp.einsum('ij,fjxyz->fixyz', blocked_stiffness[out_corner, :, in_corner, :], corner_values, precision=lax.Precision.HIGHEST)
        forces = forces * stiffness_scale[None, None]
        summed = summed.at[:, :, out_x:out_x + NX, out_y:out_y + NY, out_z:out_z + NZ].add(forces)
    return summed[:, :, :NX, :NY, :NZ]

def per_frame(values):
    return values[:, None, None, None, None]

def frame_sums(left, right):
    return lax.optimization_barrier(jnp.sum(left * right, axis=(1, 2, 3, 4)))

def reference(occupancy, modulus, displacement_start, direction_start, muscle_force, muscle_direction, attachment_nodes):
    stiffness = jnp.asarray(element_matrix(), dtype=jnp.float32)
    blocked_stiffness = stiffness.reshape(8, 3, 8, 3)
    diagonal_terms = jnp.diagonal(stiffness).reshape(8, 3)
    bone = occupancy.astype(jnp.float32)
    stiffness_scale = bone * modulus + (1.0 - bone) * ersatz_modulus
    summed = jnp.zeros((1, 3, NX + 1, NY + 1, NZ + 1), jnp.float32)
    for corner, (step_x, step_y, step_z) in enumerate(corner_offsets()):
        terms = stiffness_scale[None, None] * diagonal_terms[corner][None, :, None, None, None]
        summed = summed.at[:, :, step_x:step_x + NX, step_y:step_y + NY, step_z:step_z + NZ].add(terms)
    diagonal = summed[:, :, :NX, :NY, :NZ]
    node_x = attachment_nodes[:, :, 0].reshape(-1)
    node_y = attachment_nodes[:, :, 1].reshape(-1)
    node_z = attachment_nodes[:, :, 2].reshape(-1)
    muscle_loads = muscle_force[:, :, None] * muscle_direction / ATTACH
    values = jnp.broadcast_to(jnp.transpose(muscle_loads, (0, 2, 1))[:, :, :, None], (FRAMES, 3, MUSCLES, ATTACH)).reshape(FRAMES, 3, MUSCLES * ATTACH)
    load_field = jnp.zeros((FRAMES, 3, NX, NY, NZ), jnp.float32).at[:, :, node_x, node_y, node_z].add(values)
    displacement = displacement_start
    residual = load_field - apply_stiffness(displacement_start, stiffness_scale, blocked_stiffness)
    preconditioned = residual / diagonal
    direction = direction_start
    weighted = frame_sums(residual, preconditioned)
    for iteration in range(ITERS):
        stiff_image = apply_stiffness(direction, stiffness_scale, blocked_stiffness)
        curvature = frame_sums(direction, stiff_image)
        step_length = weighted / curvature
        displacement = displacement + per_frame(step_length) * direction
        residual = residual - per_frame(step_length) * stiff_image
        if iteration + 1 < ITERS:
            preconditioned = residual / diagonal
            weighted_next = frame_sums(residual, preconditioned)
            direction = preconditioned + per_frame(weighted_next / weighted) * direction
            weighted = weighted_next
    gathered = displacement[:, :, node_x, node_y, node_z].reshape(FRAMES, 3, MUSCLES, ATTACH)
    sensitivity = jnp.einsum('fmc,fcma->fm', muscle_direction, gathered, precision=lax.Precision.HIGHEST) / ATTACH
    return (displacement, sensitivity)
```

```python
import functools
import math

import jax
import jax.numpy as jnp
import numpy as np
from jax import lax
from jax.experimental import pallas as pl
from jax.experimental.pallas import tpu as pltpu
from jax.sharding import PartitionSpec as P

MUSCLES = 40
ATTACH = 128
FRAMES = 2
LANES = 128

ersatz_modulus = 0.02
MESH = pl.DeviceIdType.MESH
HIGHEST = lax.Precision.HIGHEST
DIRECTIONS = [(dx, dy) for dx in (-1, 0, 1) for dy in (-1, 0, 1) if (dx, dy) != (0, 0)]
LOWER = [(-1, 0), (0, -1), (-1, -1)]


def corner_offsets():
    return [(step_x, step_y, step_z) for step_x in (0, 1) for step_y in (0, 1) for step_z in (0, 1)]


def element_matrix():
    poisson = 0.3
    lame_first = poisson / ((1.0 + poisson) * (1.0 - 2.0 * poisson))
    shear_modulus = 0.5 / (1.0 + poisson)
    elastic = np.zeros((6, 6))
    elastic[:3, :3] = lame_first
    for position in range(3):
        elastic[position, position] += 2.0 * shear_modulus
        elastic[position + 3, position + 3] = shear_modulus
    points = [0.5 - 0.5 / math.sqrt(3.0), 0.5 + 0.5 / math.sqrt(3.0)]
    matrix = np.zeros((24, 24))
    for point_x in points:
        for point_y in points:
            for point_z in points:
                strain = np.zeros((6, 24))
                for corner, (step_x, step_y, step_z) in enumerate(corner_offsets()):
                    weight_x = point_x if step_x else 1.0 - point_x
                    weight_y = point_y if step_y else 1.0 - point_y
                    weight_z = point_z if step_z else 1.0 - point_z
                    sign_x = 1.0 if step_x else -1.0
                    sign_y = 1.0 if step_y else -1.0
                    sign_z = 1.0 if step_z else -1.0
                    grad_x = sign_x * weight_y * weight_z
                    grad_y = weight_x * sign_y * weight_z
                    grad_z = weight_x * weight_y * sign_z
                    column = 3 * corner
                    strain[0, column] = grad_x
                    strain[1, column + 1] = grad_y
                    strain[2, column + 2] = grad_z
                    strain[3, column] = grad_y
                    strain[3, column + 1] = grad_x
                    strain[4, column + 1] = grad_z
                    strain[4, column + 2] = grad_y
                    strain[5, column] = grad_z
                    strain[5, column + 2] = grad_x
                matrix += strain.T @ elastic @ strain / 8.0
    return matrix


def mode_terms():
    corners = corner_offsets()
    signs = np.array(
        [
            [np.prod([1.0 if (not m or s) else -1.0 for m, s in zip(mode, step)]) for step in corners]
            for mode in corners
        ]
    )
    matrix = element_matrix().reshape(8, 3, 8, 3)
    modal = np.einsum("ma,aibj,nb->minj", signs, matrix, signs) / 64.0
    terms = {}
    for m, mode in enumerate(corners):
        for i in range(3):
            row = [
                ((j,) + corners[n], float(modal[m, i, n, j]))
                for n in range(8)
                for j in range(3)
                if abs(modal[m, i, n, j]) > 1e-9
            ]
            if row:
                terms[(i,) + mode] = row
    return terms


TERMS = mode_terms()
DIAGONAL = float(element_matrix()[0, 0])


def apply_modes(modes):
    forces = {}
    for key, row in TERMS.items():
        total = None
        for other, value in row:
            term = modes[other] * value
            total = term if total is None else total + term
        forces[key] = total
    return forces


def split_rows(values):
    high = values.astype(jnp.bfloat16)
    low = (values - high.astype(jnp.float32)).astype(jnp.bfloat16)
    return jnp.concatenate([high, low], axis=0)


def kernel(
    slabs,
    bricks,
    occ_ref,
    mod_ref,
    start_ref,
    dir_ref,
    force_ref,
    line_ref,
    att_ref,
    out_ref,
    sens_ref,
    ext,
    image,
    carry_x,
    pair,
    load,
    counts,
    slab_part,
    brick_part,
    halo_send,
    halo_recv,
    pair_send,
    pair_recv,
    slab_send,
    slab_recv,
    brick_send,
    brick_recv,
):
    size_x, size_y, size_z = occ_ref.shape
    tiles = size_z // LANES
    rows = FRAMES * tiles
    slab = lax.axis_index("slab")
    brick = lax.axis_index("brick")
    barrier = pltpu.get_barrier_semaphore()

    def present(dx, dy):
        ok = None
        for delta, place, count in ((dx, slab, slabs), (dy, brick, bricks)):
            if delta == 0:
                continue
            here = (place > 0) if delta < 0 else (place < count - 1)
            ok = here if ok is None else ok & here
        return ok

    for step in range(1, slabs):
        pl.semaphore_signal(
            barrier, inc=1, device_id=(lax.rem(slab + step, slabs), brick), device_id_type=MESH
        )
    for step in range(1, bricks):
        pl.semaphore_signal(
            barrier, inc=1, device_id=(slab, lax.rem(brick + step, bricks)), device_id_type=MESH
        )
    for dx, dy in DIRECTIONS:
        if dx and dy:

            @pl.when(present(dx, dy))
            def _():
                pl.semaphore_signal(
                    barrier, inc=1, device_id=(slab + dx, brick + dy), device_id_type=MESH
                )

    flat = ext.reshape(7 * (size_x + 2) * (size_y + 2) * rows, LANES)
    zero = jnp.zeros((rows, LANES), jnp.float32)

    def place(field, x, row, value):
        base = ((field * (size_x + 2) + x + 1) * (size_y + 2) + 1) * rows + row
        flat[pl.ds(base, size_y, stride=rows), :] = value

    for x in range(size_x):
        for tile in range(tiles):
            part = slice(tile * LANES, (tile + 1) * LANES)
            bone = occ_ref[x, :, part].astype(jnp.float32)
            scale = bone * mod_ref[x, :, part] + (1.0 - bone) * ersatz_modulus
            for frame in range(FRAMES):
                row = frame * tiles + tile
                place(6, x, row, scale)
                for c in range(3):
                    place(c, x, row, start_ref[frame, c, x, :, part])
                    place(3 + c, x, row, dir_ref[frame, c, x, :, part])

    def edge(delta, size):
        if delta == 0:
            return pl.ds(1, size), pl.ds(1, size)
        return (pl.ds(1, 1), pl.ds(size + 1, 1)) if delta < 0 else (pl.ds(size, 1), pl.ds(0, 1))

    def halo(number):
        dx, dy = DIRECTIONS[number]
        source_x, target_x = edge(dx, size_x)
        source_y, target_y = edge(dy, size_y)
        fields = pl.ds(0, 7 if dx >= 0 and dy >= 0 else 6)
        return pltpu.make_async_remote_copy(
            src_ref=ext.at[fields, source_x, source_y],
            dst_ref=ext.at[fields, target_x, target_y],
            send_sem=halo_send.at[number],
            recv_sem=halo_recv.at[number],
            device_id=(slab + dx, brick + dy),
            device_id_type=MESH,
        )

    for number, (dx, dy) in enumerate(DIRECTIONS):
        back_x, back_y = edge(dx, size_x)[1], edge(dy, size_y)[1]

        @pl.when(jnp.logical_not(present(-dx, -dy)))
        def _():
            shape = (7, back_x.size, back_y.size, rows, LANES)
            ext[:, back_x, back_y] = jnp.zeros(shape, jnp.float32)

    amount = slabs + bricks - 2
    for dx, dy in DIRECTIONS:
        if dx and dy:
            amount = amount + present(dx, dy).astype(jnp.int32)
    pl.semaphore_wait(barrier, amount)

    for number, (dx, dy) in enumerate(DIRECTIONS):

        @pl.when(present(dx, dy))
        def _():
            halo(number).start()

    width = 2 * ATTACH
    span = MUSCLES * tiles
    row_ids = lax.broadcasted_iota(jnp.int32, (size_x * size_y * 2 * tiles, width), 0)
    lane_ids = lax.broadcasted_iota(jnp.int32, (LANES, width), 0)
    second = (lax.broadcasted_iota(jnp.int32, (1, width), 1) >= ATTACH).astype(jnp.int32)

    @pl.loop(0, MUSCLES // 2)
    def _(two):
        def both(dim):
            return jnp.concatenate(
                [att_ref[dim, pl.ds(2 * two, 1), :], att_ref[dim, pl.ds(2 * two + 1, 1), :]], axis=1
            )

        near_x = both(0) - slab * size_x
        near_y = both(1) - brick * size_y
        far = both(2)
        tile = lax.shift_right_logical(far, 7)
        inside = (near_x >= 0) & (near_x < size_x) & (near_y >= 0) & (near_y < size_y)
        code = ((near_x * size_y + near_y) * 2 + second) * tiles + tile
        code = jnp.where(inside, code, -1)
        hits = jnp.where(row_ids == code, 1.0, 0.0).astype(jnp.bfloat16)
        depth = jnp.where(lane_ids == far - tile * LANES, 1.0, 0.0).astype(jnp.bfloat16)
        found = lax.dot_general(
            hits, depth, (((1,), (1,)), ((), ())), preferred_element_type=jnp.float32
        )
        counts[:, pl.ds(pl.multiple_of(two * 2 * tiles, 8), 2 * tiles), :] = found.reshape(
            size_x * size_y, 2 * tiles, LANES
        )

    def iota(shape, dim):
        return lax.broadcasted_iota(jnp.int32, shape, dim)

    def dot32(left, right):
        return jnp.dot(left, right, precision=HIGHEST, preferred_element_type=jnp.float32)

    def ones_where(mask):
        return jnp.where(mask, 1.0, 0.0)

    spread_rows = ones_where(iota((24, 6), 0) // tiles == iota((24, 6), 1))
    spread_cols = ones_where(iota((MUSCLES, span), 1) // tiles == iota((MUSCLES, span), 0))
    same_tile = ones_where(iota((24, span), 0) % tiles == iota((24, span), 1) % tiles)
    lines = line_ref[...] * (1.0 / ATTACH)
    forces = jnp.concatenate([force_ref[...]] * 3, axis=0)
    line_wide = dot32(spread_rows, dot32(lines, spread_cols)) * same_tile
    load_wide = split_rows(dot32(spread_rows, dot32(lines * forces, spread_cols)) * same_tile)

    @pl.loop(0, size_x * size_y)
    def _(column):
        both = jnp.dot(
            load_wide, counts[column].astype(jnp.bfloat16), preferred_element_type=jnp.float32
        )
        load[column] = both[:24] + both[24:]

    def sampled(ref, offset):
        def body(column, total):
            x, y = column // size_y, column % size_y
            values = ref[pl.ds(0, 6), x + offset, y + offset].reshape(6 * rows, LANES)
            return total + lax.dot_general(
                split_rows(values),
                counts[column].astype(jnp.bfloat16),
                (((1,), (1,)), ((), ())),
                preferred_element_type=jnp.float32,
            )

        both = lax.fori_loop(
            0, size_x * size_y, body, jnp.zeros((12 * rows, span), jnp.float32)
        )
        total = (both[: 6 * rows] + both[6 * rows :]) * jnp.concatenate([line_wide] * 2, axis=0)
        shape = (4, 6 * rows)
        at = iota(shape, 1)
        pick = (at // 24 == iota(shape, 0) // 2) & ((at // tiles) % 2 == iota(shape, 0) % 2)
        narrow = ones_where(iota((span, LANES), 0) // tiles == iota((span, LANES), 1))
        return dot32(dot32(ones_where(pick), total), narrow)

    first_sums = sampled(ext, 1)

    lane = iota((rows, LANES), 1)
    tile_of = iota((rows, LANES), 0) % tiles
    is_last, is_first = lane == LANES - 1, lane == 0
    keep_up = ones_where(tile_of != tiles - 1)
    keep_down = ones_where(tile_of != 0)

    def from_above(value):
        turned = pltpu.roll(value, LANES - 1, 1)
        return jnp.where(is_last, pltpu.roll(turned, rows - 1, 0) * keep_up, turned)

    def from_below(value):
        turned = pltpu.roll(value, 1, 1)
        return jnp.where(is_first, pltpu.roll(turned, 1, 0) * keep_down, turned)

    def column_modes(ref, field, x, y):
        found = []
        for c in range(3):
            low, high = ref[field + c, x, y], ref[field + c, x + 1, y]
            for value in (high + low, high - low):
                above = from_above(value)
                found += [above + value, above - value]
        return tuple(found)

    def element_modes(before, after):
        modes = {}
        for c in range(3):
            for mx in (0, 1):
                for mz in (0, 1):
                    low, high = before[c * 4 + mx * 2 + mz], after[c * 4 + mx * 2 + mz]
                    modes[c, mx, 0, mz] = high + low
                    modes[c, mx, 1, mz] = high - low
        return modes

    for number, (dx, dy) in enumerate(DIRECTIONS):

        @pl.when(present(-dx, -dy))
        def _():
            halo(number).wait_recv()

    carry_x[...] = jnp.zeros_like(carry_x)

    @pl.loop(0, size_x + 1)
    def _(x):
        for half in (0, 1):

            def body(y, carry):
                before, pending = carry
                after = column_modes(ext, 3 * half, x, y + 1)
                forces = apply_modes(element_modes(before, after))
                scale = ext[6, x, y]
                later = []
                for c in range(3):
                    parts = []
                    for mx in (0, 1):
                        done = []
                        for mz in (0, 1):
                            odd = forces[c, mx, 1, mz] * scale
                            if (c, mx, 0, mz) in forces:
                                even = forces[c, mx, 0, mz] * scale
                                low, high = even - odd, even + odd
                            else:
                                low, high = -odd, odd
                            done.append(low + pending[c * 4 + mx * 2 + mz])
                            later.append(high)
                        parts.append((done[0] - done[1]) + from_below(done[0] + done[1]))
                    index = 3 * half + c
                    image[index, x, y] = carry_x[index, y] + (parts[0] - parts[1])
                    carry_x[index, y] = parts[0] + parts[1]
                return after, tuple(later)

            lax.fori_loop(
                0, size_y + 1, body, (column_modes(ext, 3 * half, x, 0), (zero,) * 12)
            )

    def node(column, totals):
        x, y = column // size_y, column % size_y
        around = (ext[6, x, y] + ext[6, x, y + 1]) + (ext[6, x + 1, y] + ext[6, x + 1, y + 1])
        inverse = 1.0 / ((around + from_below(around)) * DIAGONAL)
        norm, curve, cross, square = totals
        for c in range(3):
            residual = load[column, pl.ds(c * rows, rows), :] - image[c, x + 1, y + 1]
            stiff = image[3 + c, x + 1, y + 1]
            scaled, other = residual * inverse, stiff * inverse
            pair[c, x, y] = scaled
            pair[3 + c, x, y] = other
            norm = norm + residual * scaled
            curve = curve + ext[3 + c, x + 1, y + 1] * stiff
            cross = cross + residual * other
            square = square + stiff * other
        return norm, curve, cross, square

    totals = lax.fori_loop(0, size_x * size_y, node, (zero,) * 4)

    def pair_edge(delta, size):
        return (pl.ds(0, size), pl.ds(0, size)) if delta == 0 else (pl.ds(0, 1), pl.ds(size, 1))

    def pair_copy(number):
        dx, dy = LOWER[number]
        source_x, target_x = pair_edge(dx, size_x)
        source_y, target_y = pair_edge(dy, size_y)
        return pltpu.make_async_remote_copy(
            src_ref=pair.at[:, source_x, source_y],
            dst_ref=pair.at[:, target_x, target_y],
            send_sem=pair_send.at[number],
            recv_sem=pair_recv.at[number],
            device_id=(slab + dx, brick + dy),
            device_id_type=MESH,
        )

    for number, (dx, dy) in enumerate(LOWER):

        @pl.when(present(dx, dy))
        def _():
            pair_copy(number).start()

    for number, (dx, dy) in enumerate(LOWER):
        target_x, target_y = pair_edge(dx, size_x)[1], pair_edge(dy, size_y)[1]

        @pl.when(jnp.logical_not(present(-dx, -dy)))
        def _():
            shape = (6, target_x.size, target_y.size, rows, LANES)
            pair[:, target_x, target_y] = jnp.zeros(shape, jnp.float32)

    second_sums = sampled(pair, 0)

    for number, (dx, dy) in enumerate(LOWER):

        @pl.when(present(-dx, -dy))
        def _():
            pair_copy(number).wait_recv()

    def energy_row(x, energies):
        def body(y, carry):
            before, before_other, (first, mixed, last) = carry
            after = column_modes(pair, 0, x, y + 1)
            after_other = column_modes(pair, 3, x, y + 1)
            modes = element_modes(before, after)
            other = element_modes(before_other, after_other)
            scale = ext[6, x + 1, y + 1]
            forces, other_forces = apply_modes(modes), apply_modes(other)

            def dotted(left, right):
                total = None
                for key in TERMS:
                    term = left[key] * right[key]
                    total = term if total is None else total + term
                return total * scale

            first = first + dotted(modes, forces)
            mixed = mixed + dotted(other, forces)
            last = last + dotted(other, other_forces)
            return after, after_other, (first, mixed, last)

        start = (column_modes(pair, 0, x, 0), column_modes(pair, 3, x, 0), energies)
        return lax.fori_loop(0, size_y, body, start)[2]

    energies = lax.fori_loop(0, size_x, energy_row, (zero,) * 3)

    payload = jnp.concatenate([first_sums, second_sums], axis=0)
    for number, total in enumerate(totals + energies):
        payload = jnp.where(lane == 64 + number, jnp.sum(total, axis=1, keepdims=True), payload)

    def summed(value, part, me, count, send, recv, device):
        part[me] = value
        for step in range(1, count):
            pltpu.make_async_remote_copy(
                src_ref=part.at[me],
                dst_ref=part.at[me],
                send_sem=send.at[step - 1],
                recv_sem=recv.at[step - 1],
                device_id=device(lax.rem(me + step, count)),
                device_id_type=MESH,
            ).start()
        for step in range(1, count):
            source = lax.rem(me - step + count, count)
            pltpu.make_async_remote_copy(
                src_ref=part.at[source],
                dst_ref=part.at[source],
                send_sem=send.at[step - 1],
                recv_sem=recv.at[step - 1],
                device_id=device(source),
                device_id_type=MESH,
            ).wait_recv()
        total = part[0]
        for index in range(1, count):
            total = total + part[index]
        return total

    total = summed(payload, slab_part, slab, slabs, slab_send, slab_recv, lambda i: (i, brick))
    total = summed(total, brick_part, brick, bricks, brick_send, brick_recv, lambda i: (slab, i))

    frame_one = iota((rows, LANES), 0) >= tiles

    def scalar(number):
        column = total[:, 64 + number : 65 + number]
        return (
            jnp.sum(column[:tiles], axis=0, keepdims=True),
            jnp.sum(column[tiles:], axis=0, keepdims=True),
        )

    sums = [scalar(number) for number in range(7)]
    factors = []
    for frame in range(FRAMES):
        norm, curve, cross, square, first, mixed, last = [pairs[frame] for pairs in sums]
        step = norm / curve
        norm_next = norm - 2.0 * step * cross + step * step * square
        ratio = norm_next / norm
        curve_next = (
            (first - 2.0 * step * mixed + step * step * last)
            + 2.0 * ratio * (cross - step * square)
            + ratio * ratio * curve
        )
        step_next = norm_next / curve_next
        factors.append((step + step_next * ratio, step_next, -step_next * step))
    wide = [jnp.where(frame_one, factors[1][i], factors[0][i]) for i in range(3)]

    for frame in range(FRAMES):
        line = total[frame : frame + 1]
        for i in range(3):
            at = 2 * (i + 1) + frame
            line = line + factors[frame][i] * total[at : at + 1]
        sens_ref[frame : frame + 1, :] = line[:, :MUSCLES]

    flat_image = image.reshape(6 * (size_x + 1) * (size_y + 1) * rows, LANES)

    @pl.loop(0, size_x * size_y)
    def _(column):
        x, y = column // size_y, column % size_y
        for c in range(3):
            image[c, x, y] = (
                ext[c, x + 1, y + 1]
                + wide[0] * ext[3 + c, x + 1, y + 1]
                + wide[1] * pair[c, x, y]
                + wide[2] * pair[3 + c, x, y]
            )

    for frame in range(FRAMES):
        for c in range(3):
            for x in range(size_x):
                for tile in range(tiles):
                    base = (c * (size_x + 1) + x) * (size_y + 1) * rows + frame * tiles + tile
                    out_ref[frame, c, x, :, tile * LANES : (tile + 1) * LANES] = flat_image[
                        pl.ds(base, size_y, stride=rows), :
                    ]

    for number, (dx, dy) in enumerate(DIRECTIONS):

        @pl.when(present(dx, dy))
        def _():
            halo(number).wait_send()

    for number, (dx, dy) in enumerate(LOWER):

        @pl.when(present(dx, dy))
        def _():
            pair_copy(number).wait_send()

    for part, me, count, send, recv, device in (
        (slab_part, slab, slabs, slab_send, slab_recv, lambda i: (i, brick)),
        (brick_part, brick, bricks, brick_send, brick_recv, lambda i: (slab, i)),
    ):
        for step in range(1, count):
            pltpu.make_async_remote_copy(
                src_ref=part.at[me],
                dst_ref=part.at[me],
                send_sem=send.at[step - 1],
                recv_sem=recv.at[step - 1],
                device_id=device(lax.rem(me + step, count)),
                device_id_type=MESH,
            ).wait_send()


def on_device(slabs, bricks, occupancy, modulus, start, direction, force, line, attachments):
    size_x, size_y, size_z = occupancy.shape
    tiles = size_z // LANES
    rows = FRAMES * tiles
    vmem = pl.BlockSpec(memory_space=pltpu.VMEM)
    dma = pltpu.SemaphoreType.DMA
    return pl.pallas_call(
        functools.partial(kernel, slabs, bricks),
        out_shape=(
            jax.ShapeDtypeStruct(start.shape, jnp.float32),
            jax.ShapeDtypeStruct(force.shape, jnp.float32),
        ),
        in_specs=[vmem] * 7,
        out_specs=(vmem, vmem),
        scratch_shapes=[
            pltpu.VMEM((7, size_x + 2, size_y + 2, rows, LANES), jnp.float32),
            pltpu.VMEM((6, size_x + 1, size_y + 1, rows, LANES), jnp.float32),
            pltpu.VMEM((6, size_y + 1, rows, LANES), jnp.float32),
            pltpu.VMEM((6, size_x + 1, size_y + 1, rows, LANES), jnp.float32),
            pltpu.VMEM((size_x * size_y, 3 * rows, LANES), jnp.float32),
            pltpu.VMEM((size_x * size_y, MUSCLES * tiles, LANES), jnp.float32),
            pltpu.VMEM((slabs, rows, LANES), jnp.float32),
            pltpu.VMEM((bricks, rows, LANES), jnp.float32),
            dma((8,)),
            dma((8,)),
            dma((3,)),
            dma((3,)),
            dma((slabs - 1,)),
            dma((slabs - 1,)),
            dma((bricks - 1,)),
            dma((bricks - 1,)),
        ],
        compiler_params=pltpu.CompilerParams(
            collective_id=0, has_side_effects=True, vmem_limit_bytes=40 * 1024 * 1024
        ),
    )(
        occupancy,
        modulus,
        start,
        direction,
        force,
        jnp.transpose(line, (2, 0, 1)).reshape(3 * FRAMES, MUSCLES),
        jnp.transpose(attachments, (2, 0, 1)),
    )


def solution(mesh):
    return jax.shard_map(
        functools.partial(on_device, mesh.shape["slab"], mesh.shape["brick"]),
        mesh=mesh,
        in_specs=(
            P("slab", "brick", None),
            P("slab", "brick", None),
            P(None, None, "slab", "brick", None),
            P(None, None, "slab", "brick", None),
            P(),
            P(),
            P(),
        ),
        out_specs=(P(None, None, "slab", "brick", None), P()),
        check_vma=False,
    )
```

```python
import functools
import math

import jax
import jax.numpy as jnp
import numpy as np
from jax import lax
from jax.experimental import pallas as pl
from jax.experimental.pallas import tpu as pltpu
from jax.sharding import PartitionSpec as P

MUSCLES = 40
ATTACH = 128
FRAMES = 2
LANES = 128
UNROLL_IMAGE = 3
UNROLL_ENERGY = 4

ersatz_modulus = 0.02
MESH = pl.DeviceIdType.MESH
HIGHEST = lax.Precision.HIGHEST
DIRECTIONS = [(dx, dy) for dx in (-1, 0, 1) for dy in (-1, 0, 1) if (dx, dy) != (0, 0)]
LOWER = [(-1, 0), (0, -1), (-1, -1)]


def corner_offsets():
    return [(step_x, step_y, step_z) for step_x in (0, 1) for step_y in (0, 1) for step_z in (0, 1)]


def element_matrix():
    poisson = 0.3
    lame_first = poisson / ((1.0 + poisson) * (1.0 - 2.0 * poisson))
    shear_modulus = 0.5 / (1.0 + poisson)
    elastic = np.zeros((6, 6))
    elastic[:3, :3] = lame_first
    for position in range(3):
        elastic[position, position] += 2.0 * shear_modulus
        elastic[position + 3, position + 3] = shear_modulus
    points = [0.5 - 0.5 / math.sqrt(3.0), 0.5 + 0.5 / math.sqrt(3.0)]
    matrix = np.zeros((24, 24))
    for point_x in points:
        for point_y in points:
            for point_z in points:
                strain = np.zeros((6, 24))
                for corner, (step_x, step_y, step_z) in enumerate(corner_offsets()):
                    weight_x = point_x if step_x else 1.0 - point_x
                    weight_y = point_y if step_y else 1.0 - point_y
                    weight_z = point_z if step_z else 1.0 - point_z
                    sign_x = 1.0 if step_x else -1.0
                    sign_y = 1.0 if step_y else -1.0
                    sign_z = 1.0 if step_z else -1.0
                    grad_x = sign_x * weight_y * weight_z
                    grad_y = weight_x * sign_y * weight_z
                    grad_z = weight_x * weight_y * sign_z
                    column = 3 * corner
                    strain[0, column] = grad_x
                    strain[1, column + 1] = grad_y
                    strain[2, column + 2] = grad_z
                    strain[3, column] = grad_y
                    strain[3, column + 1] = grad_x
                    strain[4, column + 1] = grad_z
                    strain[4, column + 2] = grad_y
                    strain[5, column] = grad_z
                    strain[5, column + 2] = grad_x
                matrix += strain.T @ elastic @ strain / 8.0
    return matrix


def mode_terms():
    corners = corner_offsets()
    signs = np.array(
        [
            [np.prod([1.0 if (not m or s) else -1.0 for m, s in zip(mode, step)]) for step in corners]
            for mode in corners
        ]
    )
    matrix = element_matrix().reshape(8, 3, 8, 3)
    modal = np.einsum("ma,aibj,nb->minj", signs, matrix, signs) / 64.0
    terms = {}
    for m, mode in enumerate(corners):
        for i in range(3):
            row = [
                ((j,) + corners[n], float(modal[m, i, n, j]))
                for n in range(8)
                for j in range(3)
                if abs(modal[m, i, n, j]) > 1e-9
            ]
            if row:
                terms[(i,) + mode] = row
    return terms


TERMS = mode_terms()
DIAGONAL = float(element_matrix()[0, 0])


def apply_modes(modes):
    forces = {}
    for key, row in TERMS.items():
        total = None
        for other, value in row:
            term = modes[other] * value
            total = term if total is None else total + term
        forces[key] = total
    return forces


def split_rows(values):
    high = values.astype(jnp.bfloat16)
    low = (values - high.astype(jnp.float32)).astype(jnp.bfloat16)
    return jnp.concatenate([high, low], axis=0)


def kernel(
    slabs,
    bricks,
    start_in,
    dir_in,
    occ_in,
    mod_in,
    att_in,
    force_in,
    line_in,
    out_ref,
    sens_ref,
    start_ref,
    dir_ref,
    occ_ref,
    mod_ref,
    att_ref,
    force_ref,
    line_ref,
    fetched,
    ext,
    image,
    carry_x,
    pair,
    load,
    counts,
    slab_part,
    brick_part,
    halo_send,
    halo_recv,
    pair_send,
    pair_recv,
    slab_send,
    slab_recv,
    brick_send,
    brick_recv,
):
    size_x, size_y, size_z = occ_ref.shape
    tiles = size_z // LANES
    rows = FRAMES * tiles
    slab = lax.axis_index("slab")
    brick = lax.axis_index("brick")
    barrier = pltpu.get_barrier_semaphore()
    sources = (start_in, dir_in, occ_in, mod_in, att_in, force_in, line_in)
    targets = (start_ref, dir_ref, occ_ref, mod_ref, att_ref, force_ref, line_ref)
    fetches = [
        pltpu.make_async_copy(source, target, fetched.at[number])
        for number, (source, target) in enumerate(zip(sources, targets))
    ]
    for fetch in fetches:
        fetch.start()

    def present(dx, dy):
        ok = None
        for delta, place, count in ((dx, slab, slabs), (dy, brick, bricks)):
            if delta == 0:
                continue
            here = (place > 0) if delta < 0 else (place < count - 1)
            ok = here if ok is None else ok & here
        return ok

    for step in range(1, slabs):
        pl.semaphore_signal(
            barrier, inc=1, device_id=(lax.rem(slab + step, slabs), brick), device_id_type=MESH
        )
    for step in range(1, bricks):
        pl.semaphore_signal(
            barrier, inc=1, device_id=(slab, lax.rem(brick + step, bricks)), device_id_type=MESH
        )
    for dx, dy in DIRECTIONS:
        if dx and dy:

            @pl.when(present(dx, dy))
            def _():
                pl.semaphore_signal(
                    barrier, inc=1, device_id=(slab + dx, brick + dy), device_id_type=MESH
                )

    flat = ext.reshape(7 * (size_x + 2) * (size_y + 2) * rows, LANES)
    zero = jnp.zeros((rows, LANES), jnp.float32)

    def place(field, x, row, value):
        base = ((field * (size_x + 2) + x + 1) * (size_y + 2) + 1) * rows + row
        flat[pl.ds(base, size_y, stride=rows), :] = value

    for fetch in fetches[:4]:
        fetch.wait()

    for x in range(size_x):
        for tile in range(tiles):
            part = slice(tile * LANES, (tile + 1) * LANES)
            bone = occ_ref[x, :, part].astype(jnp.float32)
            scale = bone * mod_ref[x, :, part] + (1.0 - bone) * ersatz_modulus
            for frame in range(FRAMES):
                row = frame * tiles + tile
                place(6, x, row, scale)
                for c in range(3):
                    place(c, x, row, start_ref[frame, c, x, :, part])
                    place(3 + c, x, row, dir_ref[frame, c, x, :, part])

    def edge(delta, size):
        if delta == 0:
            return pl.ds(1, size), pl.ds(1, size)
        return (pl.ds(1, 1), pl.ds(size + 1, 1)) if delta < 0 else (pl.ds(size, 1), pl.ds(0, 1))

    def halo(number):
        dx, dy = DIRECTIONS[number]
        source_x, target_x = edge(dx, size_x)
        source_y, target_y = edge(dy, size_y)
        fields = pl.ds(0, 7 if dx >= 0 and dy >= 0 else 6)
        return pltpu.make_async_remote_copy(
            src_ref=ext.at[fields, source_x, source_y],
            dst_ref=ext.at[fields, target_x, target_y],
            send_sem=halo_send.at[number],
            recv_sem=halo_recv.at[number],
            device_id=(slab + dx, brick + dy),
            device_id_type=MESH,
        )

    for number, (dx, dy) in enumerate(DIRECTIONS):
        back_x, back_y = edge(dx, size_x)[1], edge(dy, size_y)[1]

        @pl.when(jnp.logical_not(present(-dx, -dy)))
        def _():
            shape = (7, back_x.size, back_y.size, rows, LANES)
            ext[:, back_x, back_y] = jnp.zeros(shape, jnp.float32)

    amount = slabs + bricks - 2
    for dx, dy in DIRECTIONS:
        if dx and dy:
            amount = amount + present(dx, dy).astype(jnp.int32)
    pl.semaphore_wait(barrier, amount)

    for number, (dx, dy) in enumerate(DIRECTIONS):

        @pl.when(present(dx, dy))
        def _():
            halo(number).start()

    width = 2 * ATTACH
    span = MUSCLES * tiles
    row_ids = lax.broadcasted_iota(jnp.int32, (size_x * size_y * 2 * tiles, width), 0)
    lane_ids = lax.broadcasted_iota(jnp.int32, (LANES, width), 0)
    second = (lax.broadcasted_iota(jnp.int32, (1, width), 1) >= ATTACH).astype(jnp.int32)

    for fetch in fetches[4:]:
        fetch.wait()

    @pl.loop(0, MUSCLES // 2, unroll=4)
    def _(two):
        def both(dim):
            return jnp.concatenate(
                [att_ref[dim, pl.ds(2 * two, 1), :], att_ref[dim, pl.ds(2 * two + 1, 1), :]], axis=1
            )

        near_x = both(0) - slab * size_x
        near_y = both(1) - brick * size_y
        far = both(2)
        tile = lax.shift_right_logical(far, 7)
        inside = (near_x >= 0) & (near_x < size_x) & (near_y >= 0) & (near_y < size_y)
        code = ((near_x * size_y + near_y) * 2 + second) * tiles + tile
        code = jnp.where(inside, code, -1)
        hits = jnp.where(row_ids == code, 1.0, 0.0).astype(jnp.bfloat16)
        depth = jnp.where(lane_ids == far - tile * LANES, 1.0, 0.0).astype(jnp.bfloat16)
        found = lax.dot_general(
            hits, depth, (((1,), (1,)), ((), ())), preferred_element_type=jnp.float32
        )
        counts[:, pl.ds(pl.multiple_of(two * 2 * tiles, 8), 2 * tiles), :] = found.reshape(
            size_x * size_y, 2 * tiles, LANES
        )

    def iota(shape, dim):
        return lax.broadcasted_iota(jnp.int32, shape, dim)

    def dot32(left, right):
        return jnp.dot(left, right, precision=HIGHEST, preferred_element_type=jnp.float32)

    def ones_where(mask):
        return jnp.where(mask, 1.0, 0.0)

    spread_rows = ones_where(iota((24, 6), 0) // tiles == iota((24, 6), 1))
    spread_cols = ones_where(iota((MUSCLES, span), 1) // tiles == iota((MUSCLES, span), 0))
    same_tile = ones_where(iota((24, span), 0) % tiles == iota((24, span), 1) % tiles)
    lines = jnp.concatenate([line_ref[c] for c in range(3)], axis=0) * (1.0 / ATTACH)
    forces = jnp.concatenate([force_ref[...]] * 3, axis=0)
    line_wide = dot32(spread_rows, dot32(lines, spread_cols)) * same_tile
    load_wide = split_rows(dot32(spread_rows, dot32(lines * forces, spread_cols)) * same_tile)

    @pl.loop(0, size_x * size_y, unroll=8)
    def _(column):
        both = jnp.dot(
            load_wide, counts[column].astype(jnp.bfloat16), preferred_element_type=jnp.float32
        )
        load[column] = both[:24] + both[24:]

    def sampled(ref, offset):
        def body(column, total):
            x, y = column // size_y, column % size_y
            values = ref[pl.ds(0, 6), x + offset, y + offset].reshape(6 * rows, LANES)
            return total + lax.dot_general(
                split_rows(values),
                counts[column].astype(jnp.bfloat16),
                (((1,), (1,)), ((), ())),
                preferred_element_type=jnp.float32,
            )

        both = lax.fori_loop(
            0, size_x * size_y, body, jnp.zeros((12 * rows, span), jnp.float32), unroll=8
        )
        total = (both[: 6 * rows] + both[6 * rows :]) * jnp.concatenate([line_wide] * 2, axis=0)
        shape = (4, 6 * rows)
        at = iota(shape, 1)
        pick = (at // 24 == iota(shape, 0) // 2) & ((at // tiles) % 2 == iota(shape, 0) % 2)
        narrow = ones_where(iota((span, LANES), 0) // tiles == iota((span, LANES), 1))
        return dot32(dot32(ones_where(pick), total), narrow)

    first_sums = sampled(ext, 1)

    lane = iota((rows, LANES), 1)
    tile_of = iota((rows, LANES), 0) % tiles
    is_last, is_first = lane == LANES - 1, lane == 0
    keep_up = ones_where(tile_of != tiles - 1)
    keep_down = ones_where(tile_of != 0)

    def from_above(value):
        turned = pltpu.roll(value, LANES - 1, 1)
        return jnp.where(is_last, pltpu.roll(turned, rows - 1, 0) * keep_up, turned)

    def from_below(value):
        turned = pltpu.roll(value, 1, 1)
        return jnp.where(is_first, pltpu.roll(turned, 1, 0) * keep_down, turned)

    def column_modes(ref, field, x, y):
        found = []
        for c in range(3):
            low, high = ref[field + c, x, y], ref[field + c, x + 1, y]
            for value in (high + low, high - low):
                above = from_above(value)
                found += [above + value, above - value]
        return tuple(found)

    def element_modes(before, after):
        modes = {}
        for c in range(3):
            for mx in (0, 1):
                for mz in (0, 1):
                    low, high = before[c * 4 + mx * 2 + mz], after[c * 4 + mx * 2 + mz]
                    modes[c, mx, 0, mz] = high + low
                    modes[c, mx, 1, mz] = high - low
        return modes

    for number, (dx, dy) in enumerate(DIRECTIONS):

        @pl.when(present(-dx, -dy))
        def _():
            halo(number).wait_recv()

    carry_x[...] = jnp.zeros_like(carry_x)

    @pl.loop(0, size_x + 1)
    def _(x):
        def body(y, carry):
            after_both, later_both = [], []
            scale = ext[6, x, y]
            for half in (0, 1):
                before, pending = carry[0][half], carry[1][half]
                after = column_modes(ext, 3 * half, x, y + 1)
                forces = apply_modes(element_modes(before, after))
                later = []
                for c in range(3):
                    parts = []
                    for mx in (0, 1):
                        done = []
                        for mz in (0, 1):
                            odd = forces[c, mx, 1, mz] * scale
                            if (c, mx, 0, mz) in forces:
                                even = forces[c, mx, 0, mz] * scale
                                low, high = even - odd, even + odd
                            else:
                                low, high = -odd, odd
                            done.append(low + pending[c * 4 + mx * 2 + mz])
                            later.append(high)
                        parts.append((done[0] - done[1]) + from_below(done[0] + done[1]))
                    index = 3 * half + c
                    image[index, x, y] = carry_x[index, y] + (parts[0] - parts[1])
                    carry_x[index, y] = parts[0] + parts[1]
                after_both.append(after)
                later_both.append(tuple(later))
            return tuple(after_both), tuple(later_both)

        first = tuple(column_modes(ext, 3 * half, x, 0) for half in (0, 1))
        lax.fori_loop(0, size_y + 1, body, (first, ((zero,) * 12,) * 2), unroll=UNROLL_IMAGE)

    def node(column, totals):
        x, y = column // size_y, column % size_y
        around = (ext[6, x, y] + ext[6, x, y + 1]) + (ext[6, x + 1, y] + ext[6, x + 1, y + 1])
        inverse = 1.0 / ((around + from_below(around)) * DIAGONAL)
        norm, curve, cross, square = totals
        for c in range(3):
            residual = load[column, pl.ds(c * rows, rows), :] - image[c, x + 1, y + 1]
            stiff = image[3 + c, x + 1, y + 1]
            scaled, other = residual * inverse, stiff * inverse
            pair[c, x, y] = scaled
            pair[3 + c, x, y] = other
            norm = norm + residual * scaled
            curve = curve + ext[3 + c, x + 1, y + 1] * stiff
            cross = cross + residual * other
            square = square + stiff * other
        return norm, curve, cross, square

    totals = lax.fori_loop(0, size_x * size_y, node, (zero,) * 4, unroll=4)

    def pair_edge(delta, size):
        return (pl.ds(0, size), pl.ds(0, size)) if delta == 0 else (pl.ds(0, 1), pl.ds(size, 1))

    def pair_copy(number):
        dx, dy = LOWER[number]
        source_x, target_x = pair_edge(dx, size_x)
        source_y, target_y = pair_edge(dy, size_y)
        return pltpu.make_async_remote_copy(
            src_ref=pair.at[:, source_x, source_y],
            dst_ref=pair.at[:, target_x, target_y],
            send_sem=pair_send.at[number],
            recv_sem=pair_recv.at[number],
            device_id=(slab + dx, brick + dy),
            device_id_type=MESH,
        )

    for number, (dx, dy) in enumerate(LOWER):

        @pl.when(present(dx, dy))
        def _():
            pair_copy(number).start()

    for number, (dx, dy) in enumerate(LOWER):
        target_x, target_y = pair_edge(dx, size_x)[1], pair_edge(dy, size_y)[1]

        @pl.when(jnp.logical_not(present(-dx, -dy)))
        def _():
            shape = (6, target_x.size, target_y.size, rows, LANES)
            pair[:, target_x, target_y] = jnp.zeros(shape, jnp.float32)

    second_sums = sampled(pair, 0)

    for number, (dx, dy) in enumerate(LOWER):

        @pl.when(present(-dx, -dy))
        def _():
            pair_copy(number).wait_recv()

    def energy_row(x, energies):
        def body(y, carry):
            before, before_other, (first, mixed, last) = carry
            after = column_modes(pair, 0, x, y + 1)
            after_other = column_modes(pair, 3, x, y + 1)
            modes = element_modes(before, after)
            other = element_modes(before_other, after_other)
            scale = ext[6, x + 1, y + 1]
            forces, other_forces = apply_modes(modes), apply_modes(other)

            def dotted(left, right):
                total = None
                for key in TERMS:
                    term = left[key] * right[key]
                    total = term if total is None else total + term
                return total * scale

            first = first + dotted(modes, forces)
            mixed = mixed + dotted(other, forces)
            last = last + dotted(other, other_forces)
            return after, after_other, (first, mixed, last)

        start = (column_modes(pair, 0, x, 0), column_modes(pair, 3, x, 0), energies)
        return lax.fori_loop(0, size_y, body, start, unroll=UNROLL_ENERGY)[2]

    energies = lax.fori_loop(0, size_x, energy_row, (zero,) * 3)

    payload = jnp.concatenate([first_sums, second_sums], axis=0)
    for number, total in enumerate(totals + energies):
        payload = jnp.where(lane == 64 + number, jnp.sum(total, axis=1, keepdims=True), payload)

    def summed(value, part, me, count, send, recv, device):
        part[me] = value
        for step in range(1, count):
            pltpu.make_async_remote_copy(
                src_ref=part.at[me],
                dst_ref=part.at[me],
                send_sem=send.at[step - 1],
                recv_sem=recv.at[step - 1],
                device_id=device(lax.rem(me + step, count)),
                device_id_type=MESH,
            ).start()
        for step in range(1, count):
            source = lax.rem(me - step + count, count)
            pltpu.make_async_remote_copy(
                src_ref=part.at[source],
                dst_ref=part.at[source],
                send_sem=send.at[step - 1],
                recv_sem=recv.at[step - 1],
                device_id=device(source),
                device_id_type=MESH,
            ).wait_recv()
        total = part[0]
        for index in range(1, count):
            total = total + part[index]
        return total

    total = summed(payload, slab_part, slab, slabs, slab_send, slab_recv, lambda i: (i, brick))
    total = summed(total, brick_part, brick, bricks, brick_send, brick_recv, lambda i: (slab, i))

    frame_one = iota((rows, LANES), 0) >= tiles

    def scalar(number):
        column = total[:, 64 + number : 65 + number]
        return (
            jnp.sum(column[:tiles], axis=0, keepdims=True),
            jnp.sum(column[tiles:], axis=0, keepdims=True),
        )

    sums = [scalar(number) for number in range(7)]
    factors = []
    for frame in range(FRAMES):
        norm, curve, cross, square, first, mixed, last = [pairs[frame] for pairs in sums]
        step = norm / curve
        norm_next = norm - 2.0 * step * cross + step * step * square
        ratio = norm_next / norm
        curve_next = (
            (first - 2.0 * step * mixed + step * step * last)
            + 2.0 * ratio * (cross - step * square)
            + ratio * ratio * curve
        )
        step_next = norm_next / curve_next
        factors.append((step + step_next * ratio, step_next, -step_next * step))
    wide = [jnp.where(frame_one, factors[1][i], factors[0][i]) for i in range(3)]

    for frame in range(FRAMES):
        line = total[frame : frame + 1]
        for i in range(3):
            at = 2 * (i + 1) + frame
            line = line + factors[frame][i] * total[at : at + 1]
        sens_ref[frame : frame + 1, :] = line[:, :MUSCLES]

    flat_image = image.reshape(6 * (size_x + 1) * (size_y + 1) * rows, LANES)

    @pl.loop(0, size_x * size_y, unroll=4)
    def _(column):
        x, y = column // size_y, column % size_y
        for c in range(3):
            image[c, x, y] = (
                ext[c, x + 1, y + 1]
                + wide[0] * ext[3 + c, x + 1, y + 1]
                + wide[1] * pair[c, x, y]
                + wide[2] * pair[3 + c, x, y]
            )

    for frame in range(FRAMES):
        for c in range(3):
            for x in range(size_x):
                for tile in range(tiles):
                    base = (c * (size_x + 1) + x) * (size_y + 1) * rows + frame * tiles + tile
                    out_ref[frame, c, x, :, tile * LANES : (tile + 1) * LANES] = flat_image[
                        pl.ds(base, size_y, stride=rows), :
                    ]

    for number, (dx, dy) in enumerate(DIRECTIONS):

        @pl.when(present(dx, dy))
        def _():
            halo(number).wait_send()

    for number, (dx, dy) in enumerate(LOWER):

        @pl.when(present(dx, dy))
        def _():
            pair_copy(number).wait_send()

    for part, me, count, send, recv, device in (
        (slab_part, slab, slabs, slab_send, slab_recv, lambda i: (i, brick)),
        (brick_part, brick, bricks, brick_send, brick_recv, lambda i: (slab, i)),
    ):
        for step in range(1, count):
            pltpu.make_async_remote_copy(
                src_ref=part.at[me],
                dst_ref=part.at[me],
                send_sem=send.at[step - 1],
                recv_sem=recv.at[step - 1],
                device_id=device(lax.rem(me + step, count)),
                device_id_type=MESH,
            ).wait_send()


def on_device(slabs, bricks, occupancy, modulus, start, direction, force, line, attachments):
    size_x, size_y, size_z = occupancy.shape
    tiles = size_z // LANES
    rows = FRAMES * tiles
    vmem = pl.BlockSpec(memory_space=pltpu.VMEM)
    dma = pltpu.SemaphoreType.DMA
    return pl.pallas_call(
        functools.partial(kernel, slabs, bricks),
        out_shape=(
            jax.ShapeDtypeStruct(start.shape, jnp.float32),
            jax.ShapeDtypeStruct(force.shape, jnp.float32),
        ),
        in_specs=[pl.BlockSpec(memory_space=pltpu.HBM)] * 7,
        out_specs=(vmem, vmem),
        scratch_shapes=[
            pltpu.VMEM(start.shape, jnp.float32),
            pltpu.VMEM(start.shape, jnp.float32),
            pltpu.VMEM(occupancy.shape, jnp.int32),
            pltpu.VMEM(occupancy.shape, jnp.float32),
            pltpu.VMEM((3, MUSCLES, ATTACH), jnp.int32),
            pltpu.VMEM((FRAMES, MUSCLES), jnp.float32),
            pltpu.VMEM((3, FRAMES, MUSCLES), jnp.float32),
            dma((7,)),
            pltpu.VMEM((7, size_x + 2, size_y + 2, rows, LANES), jnp.float32),
            pltpu.VMEM((6, size_x + 1, size_y + 1, rows, LANES), jnp.float32),
            pltpu.VMEM((6, size_y + 1, rows, LANES), jnp.float32),
            pltpu.VMEM((6, size_x + 1, size_y + 1, rows, LANES), jnp.float32),
            pltpu.VMEM((size_x * size_y, 3 * rows, LANES), jnp.float32),
            pltpu.VMEM((size_x * size_y, MUSCLES * tiles, LANES), jnp.float32),
            pltpu.VMEM((slabs, rows, LANES), jnp.float32),
            pltpu.VMEM((bricks, rows, LANES), jnp.float32),
            dma((8,)),
            dma((8,)),
            dma((3,)),
            dma((3,)),
            dma((slabs - 1,)),
            dma((slabs - 1,)),
            dma((bricks - 1,)),
            dma((bricks - 1,)),
        ],
        compiler_params=pltpu.CompilerParams(
            collective_id=0, has_side_effects=True, vmem_limit_bytes=60 * 1024 * 1024
        ),
    )(
        start,
        direction,
        occupancy,
        modulus,
        jnp.transpose(attachments, (2, 0, 1)),
        force,
        jnp.transpose(line, (2, 0, 1)),
    )


def solution(mesh):
    return jax.shard_map(
        functools.partial(on_device, mesh.shape["slab"], mesh.shape["brick"]),
        mesh=mesh,
        in_specs=(
            P("slab", "brick", None),
            P("slab", "brick", None),
            P(None, None, "slab", "brick", None),
            P(None, None, "slab", "brick", None),
            P(),
            P(),
            P(),
        ),
        out_specs=(P(None, None, "slab", "brick", None), P()),
        check_vma=False,
    )
```

```python
import functools
import math

import jax
import jax.numpy as jnp
import numpy as np
from jax import lax
from jax.experimental import pallas as pl
from jax.experimental.pallas import tpu as pltpu
from jax.sharding import PartitionSpec as P

MUSCLES = 40
ATTACH = 128
FRAMES = 2
LANES = 128
UNROLL_IMAGE = 3
UNROLL_ENERGY = 4

ersatz_modulus = 0.02
MESH = pl.DeviceIdType.MESH
HIGHEST = lax.Precision.HIGHEST
DIRECTIONS = [(dx, dy) for dx in (-1, 0, 1) for dy in (-1, 0, 1) if (dx, dy) != (0, 0)]
LOWER = [(-1, 0), (0, -1), (-1, -1)]


def corner_offsets():
    return [(step_x, step_y, step_z) for step_x in (0, 1) for step_y in (0, 1) for step_z in (0, 1)]


def element_matrix():
    poisson = 0.3
    lame_first = poisson / ((1.0 + poisson) * (1.0 - 2.0 * poisson))
    shear_modulus = 0.5 / (1.0 + poisson)
    elastic = np.zeros((6, 6))
    elastic[:3, :3] = lame_first
    for position in range(3):
        elastic[position, position] += 2.0 * shear_modulus
        elastic[position + 3, position + 3] = shear_modulus
    points = [0.5 - 0.5 / math.sqrt(3.0), 0.5 + 0.5 / math.sqrt(3.0)]
    matrix = np.zeros((24, 24))
    for point_x in points:
        for point_y in points:
            for point_z in points:
                strain = np.zeros((6, 24))
                for corner, (step_x, step_y, step_z) in enumerate(corner_offsets()):
                    weight_x = point_x if step_x else 1.0 - point_x
                    weight_y = point_y if step_y else 1.0 - point_y
                    weight_z = point_z if step_z else 1.0 - point_z
                    sign_x = 1.0 if step_x else -1.0
                    sign_y = 1.0 if step_y else -1.0
                    sign_z = 1.0 if step_z else -1.0
                    grad_x = sign_x * weight_y * weight_z
                    grad_y = weight_x * sign_y * weight_z
                    grad_z = weight_x * weight_y * sign_z
                    column = 3 * corner
                    strain[0, column] = grad_x
                    strain[1, column + 1] = grad_y
                    strain[2, column + 2] = grad_z
                    strain[3, column] = grad_y
                    strain[3, column + 1] = grad_x
                    strain[4, column + 1] = grad_z
                    strain[4, column + 2] = grad_y
                    strain[5, column] = grad_z
                    strain[5, column + 2] = grad_x
                matrix += strain.T @ elastic @ strain / 8.0
    return matrix


def mode_terms():
    corners = corner_offsets()
    signs = np.array(
        [
            [np.prod([1.0 if (not m or s) else -1.0 for m, s in zip(mode, step)]) for step in corners]
            for mode in corners
        ]
    )
    matrix = element_matrix().reshape(8, 3, 8, 3)
    modal = np.einsum("ma,aibj,nb->minj", signs, matrix, signs) / 64.0
    terms = {}
    for m, mode in enumerate(corners):
        for i in range(3):
            row = [
                ((j,) + corners[n], float(modal[m, i, n, j]))
                for n in range(8)
                for j in range(3)
                if abs(modal[m, i, n, j]) > 1e-9
            ]
            if row:
                terms[(i,) + mode] = row
    return terms


TERMS = mode_terms()
DIAGONAL = float(element_matrix()[0, 0])


def apply_modes(modes):
    forces = {}
    for key, row in TERMS.items():
        total = None
        for other, value in row:
            term = modes[other] * value
            total = term if total is None else total + term
        forces[key] = total
    return forces


def split_rows(values):
    high = values.astype(jnp.bfloat16)
    low = (values - high.astype(jnp.float32)).astype(jnp.bfloat16)
    return jnp.concatenate([high, low], axis=0)


def kernel(
    slabs,
    bricks,
    start_in,
    dir_in,
    occ_in,
    mod_in,
    att_in,
    force_in,
    line_in,
    out_ref,
    sens_ref,
    start_ref,
    dir_ref,
    occ_ref,
    mod_ref,
    att_ref,
    force_ref,
    line_ref,
    fetched,
    ext,
    image,
    carry_x,
    pair,
    load,
    counts,
    slab_part,
    brick_part,
    halo_send,
    halo_recv,
    pair_send,
    pair_recv,
    slab_send,
    slab_recv,
    brick_send,
    brick_recv,
):
    size_x, size_y, size_z = occ_ref.shape
    tiles = size_z // LANES
    rows = FRAMES * tiles
    slab = lax.axis_index("slab")
    brick = lax.axis_index("brick")
    barrier = pltpu.get_barrier_semaphore()
    sources = (start_in, dir_in, occ_in, mod_in, att_in, force_in, line_in)
    targets = (start_ref, dir_ref, occ_ref, mod_ref, att_ref, force_ref, line_ref)
    fetches = [
        pltpu.make_async_copy(source, target, fetched.at[number])
        for number, (source, target) in enumerate(zip(sources, targets))
    ]
    for fetch in fetches:
        fetch.start()

    def present(dx, dy):
        ok = None
        for delta, place, count in ((dx, slab, slabs), (dy, brick, bricks)):
            if delta == 0:
                continue
            here = (place > 0) if delta < 0 else (place < count - 1)
            ok = here if ok is None else ok & here
        return ok

    for step in range(1, slabs):
        pl.semaphore_signal(
            barrier, inc=1, device_id=(lax.rem(slab + step, slabs), brick), device_id_type=MESH
        )
    for step in range(1, bricks):
        pl.semaphore_signal(
            barrier, inc=1, device_id=(slab, lax.rem(brick + step, bricks)), device_id_type=MESH
        )
    for dx, dy in DIRECTIONS:
        if dx and dy:

            @pl.when(present(dx, dy))
            def _():
                pl.semaphore_signal(
                    barrier, inc=1, device_id=(slab + dx, brick + dy), device_id_type=MESH
                )

    flat = ext.reshape(7 * (size_x + 2) * (size_y + 2) * rows, LANES)
    zero = jnp.zeros((rows, LANES), jnp.float32)

    def place(field, x, row, value):
        base = ((field * (size_x + 2) + x + 1) * (size_y + 2) + 1) * rows + row
        flat[pl.ds(base, size_y, stride=rows), :] = value

    for fetch in fetches[:4]:
        fetch.wait()

    for x in range(size_x):
        for tile in range(tiles):
            part = slice(tile * LANES, (tile + 1) * LANES)
            bone = occ_ref[x, :, part].astype(jnp.float32)
            scale = bone * mod_ref[x, :, part] + (1.0 - bone) * ersatz_modulus
            for frame in range(FRAMES):
                row = frame * tiles + tile
                place(6, x, row, scale)
                for c in range(3):
                    place(c, x, row, start_ref[frame, c, x, :, part])
                    place(3 + c, x, row, dir_ref[frame, c, x, :, part])

    def edge(delta, size):
        if delta == 0:
            return pl.ds(1, size), pl.ds(1, size)
        return (pl.ds(1, 1), pl.ds(size + 1, 1)) if delta < 0 else (pl.ds(size, 1), pl.ds(0, 1))

    def halo(number):
        dx, dy = DIRECTIONS[number]
        source_x, target_x = edge(dx, size_x)
        source_y, target_y = edge(dy, size_y)
        fields = pl.ds(0, 7 if dx >= 0 and dy >= 0 else 6)
        return pltpu.make_async_remote_copy(
            src_ref=ext.at[fields, source_x, source_y],
            dst_ref=ext.at[fields, target_x, target_y],
            send_sem=halo_send.at[number],
            recv_sem=halo_recv.at[number],
            device_id=(slab + dx, brick + dy),
            device_id_type=MESH,
        )

    for number, (dx, dy) in enumerate(DIRECTIONS):
        back_x, back_y = edge(dx, size_x)[1], edge(dy, size_y)[1]

        @pl.when(jnp.logical_not(present(-dx, -dy)))
        def _():
            shape = (7, back_x.size, back_y.size, rows, LANES)
            ext[:, back_x, back_y] = jnp.zeros(shape, jnp.float32)

    amount = slabs + bricks - 2
    for dx, dy in DIRECTIONS:
        if dx and dy:
            amount = amount + present(dx, dy).astype(jnp.int32)
    pl.semaphore_wait(barrier, amount)

    for number, (dx, dy) in enumerate(DIRECTIONS):

        @pl.when(present(dx, dy))
        def _():
            halo(number).start()

    width = 2 * ATTACH
    span = MUSCLES * tiles
    row_ids = lax.broadcasted_iota(jnp.int32, (size_x * size_y * 2 * tiles, width), 0)
    lane_ids = lax.broadcasted_iota(jnp.int32, (LANES, width), 0)
    second = (lax.broadcasted_iota(jnp.int32, (1, width), 1) >= ATTACH).astype(jnp.int32)

    for fetch in fetches[4:]:
        fetch.wait()

    @pl.loop(0, MUSCLES // 2, unroll=4)
    def _(two):
        def both(dim):
            return jnp.concatenate(
                [att_ref[dim, pl.ds(2 * two, 1), :], att_ref[dim, pl.ds(2 * two + 1, 1), :]], axis=1
            )

        near_x = both(0) - slab * size_x
        near_y = both(1) - brick * size_y
        far = both(2)
        tile = lax.shift_right_logical(far, 7)
        inside = (near_x >= 0) & (near_x < size_x) & (near_y >= 0) & (near_y < size_y)
        code = ((near_x * size_y + near_y) * 2 + second) * tiles + tile
        code = jnp.where(inside, code, -1)
        hits = jnp.where(row_ids == code, 1.0, 0.0).astype(jnp.bfloat16)
        depth = jnp.where(lane_ids == far - tile * LANES, 1.0, 0.0).astype(jnp.bfloat16)
        found = lax.dot_general(
            hits, depth, (((1,), (1,)), ((), ())), preferred_element_type=jnp.float32
        )
        counts[:, pl.ds(pl.multiple_of(two * 2 * tiles, 8), 2 * tiles), :] = found.reshape(
            size_x * size_y, 2 * tiles, LANES
        )

    def iota(shape, dim):
        return lax.broadcasted_iota(jnp.int32, shape, dim)

    def dot32(left, right):
        return jnp.dot(left, right, precision=HIGHEST, preferred_element_type=jnp.float32)

    def ones_where(mask):
        return jnp.where(mask, 1.0, 0.0)

    spread_rows = ones_where(iota((24, 6), 0) // tiles == iota((24, 6), 1))
    spread_cols = ones_where(iota((MUSCLES, span), 1) // tiles == iota((MUSCLES, span), 0))
    same_tile = ones_where(iota((24, span), 0) % tiles == iota((24, span), 1) % tiles)
    lines = jnp.concatenate([line_ref[c] for c in range(3)], axis=0) * (1.0 / ATTACH)
    forces = jnp.concatenate([force_ref[...]] * 3, axis=0)
    line_wide = dot32(spread_rows, dot32(lines, spread_cols)) * same_tile
    load_wide = split_rows(dot32(spread_rows, dot32(lines * forces, spread_cols)) * same_tile)

    @pl.loop(0, size_x * size_y, unroll=8)
    def _(column):
        both = jnp.dot(
            load_wide, counts[column].astype(jnp.bfloat16), preferred_element_type=jnp.float32
        )
        load[column] = both[:24] + both[24:]

    def sampled(ref, offset):
        def body(column, total):
            x, y = column // size_y, column % size_y
            values = ref[pl.ds(0, 6), x + offset, y + offset].reshape(6 * rows, LANES)
            return total + lax.dot_general(
                split_rows(values),
                counts[column].astype(jnp.bfloat16),
                (((1,), (1,)), ((), ())),
                preferred_element_type=jnp.float32,
            )

        both = lax.fori_loop(
            0, size_x * size_y, body, jnp.zeros((12 * rows, span), jnp.float32), unroll=8
        )
        total = (both[: 6 * rows] + both[6 * rows :]) * jnp.concatenate([line_wide] * 2, axis=0)
        shape = (4, 6 * rows)
        at = iota(shape, 1)
        pick = (at // 24 == iota(shape, 0) // 2) & ((at // tiles) % 2 == iota(shape, 0) % 2)
        narrow = ones_where(iota((span, LANES), 0) // tiles == iota((span, LANES), 1))
        return dot32(dot32(ones_where(pick), total), narrow)

    first_sums = sampled(ext, 1)

    lane = iota((rows, LANES), 1)
    tile_of = iota((rows, LANES), 0) % tiles
    is_last, is_first = lane == LANES - 1, lane == 0
    keep_up = ones_where(tile_of != tiles - 1)
    keep_down = ones_where(tile_of != 0)

    def from_above(value):
        turned = pltpu.roll(value, LANES - 1, 1)
        return jnp.where(is_last, pltpu.roll(turned, rows - 1, 0) * keep_up, turned)

    def from_below(value):
        turned = pltpu.roll(value, 1, 1)
        return jnp.where(is_first, pltpu.roll(turned, 1, 0) * keep_down, turned)

    def column_modes(ref, field, x, y):
        found = []
        for c in range(3):
            low, high = ref[field + c, x, y], ref[field + c, x + 1, y]
            for value in (high + low, high - low):
                above = from_above(value)
                found += [above + value, above - value]
        return tuple(found)

    def element_modes(before, after):
        modes = {}
        for c in range(3):
            for mx in (0, 1):
                for mz in (0, 1):
                    low, high = before[c * 4 + mx * 2 + mz], after[c * 4 + mx * 2 + mz]
                    modes[c, mx, 0, mz] = high + low
                    modes[c, mx, 1, mz] = high - low
        return modes

    def wait_halos(wanted):
        for number, (dx, dy) in enumerate(DIRECTIONS):
            if dx in wanted:

                @pl.when(present(-dx, -dy))
                def _():
                    halo(number).wait_recv()

    def image_row(x, lowest=False):
        def body(y, carry):
            after_both, later_both = [], []
            scale = ext[6, x, y]
            for half in (0, 1):
                before, pending = carry[0][half], carry[1][half]
                after = column_modes(ext, 3 * half, x, y + 1)
                forces = apply_modes(element_modes(before, after))
                later = []
                for c in range(3):
                    parts = []
                    for mx in (0, 1):
                        done = []
                        for mz in (0, 1):
                            odd = forces[c, mx, 1, mz] * scale
                            if (c, mx, 0, mz) in forces:
                                even = forces[c, mx, 0, mz] * scale
                                low, high = even - odd, even + odd
                            else:
                                low, high = -odd, odd
                            done.append(low + pending[c * 4 + mx * 2 + mz])
                            later.append(high)
                        parts.append((done[0] - done[1]) + from_below(done[0] + done[1]))
                    index = 3 * half + c
                    if lowest:
                        image[index, 1, y] += parts[0] + parts[1]
                    else:
                        image[index, x, y] = carry_x[index, y] + (parts[0] - parts[1])
                        carry_x[index, y] = parts[0] + parts[1]
                after_both.append(after)
                later_both.append(tuple(later))
            return tuple(after_both), tuple(later_both)

        first = tuple(column_modes(ext, 3 * half, x, 0) for half in (0, 1))
        lax.fori_loop(0, size_y + 1, body, (first, ((zero,) * 12,) * 2), unroll=UNROLL_IMAGE)

    def node(column, totals):
        x, y = column // size_y, column % size_y
        around = (ext[6, x, y] + ext[6, x, y + 1]) + (ext[6, x + 1, y] + ext[6, x + 1, y + 1])
        inverse = 1.0 / ((around + from_below(around)) * DIAGONAL)
        norm, curve, cross, square = totals
        for c in range(3):
            residual = load[column, pl.ds(c * rows, rows), :] - image[c, x + 1, y + 1]
            stiff = image[3 + c, x + 1, y + 1]
            scaled, other = residual * inverse, stiff * inverse
            pair[c, x, y] = scaled
            pair[3 + c, x, y] = other
            norm = norm + residual * scaled
            curve = curve + ext[3 + c, x + 1, y + 1] * stiff
            cross = cross + residual * other
            square = square + stiff * other
        return norm, curve, cross, square

    def pair_edge(delta, size):
        return (pl.ds(0, size), pl.ds(0, size)) if delta == 0 else (pl.ds(0, 1), pl.ds(size, 1))

    def pair_copy(number):
        dx, dy = LOWER[number]
        source_x, target_x = pair_edge(dx, size_x)
        source_y, target_y = pair_edge(dy, size_y)
        return pltpu.make_async_remote_copy(
            src_ref=pair.at[:, source_x, source_y],
            dst_ref=pair.at[:, target_x, target_y],
            send_sem=pair_send.at[number],
            recv_sem=pair_recv.at[number],
            device_id=(slab + dx, brick + dy),
            device_id_type=MESH,
        )

    def start_pair(numbers):
        for number in numbers:

            @pl.when(present(*LOWER[number]))
            def _():
                pair_copy(number).start()

    def wait_pair(numbers):
        for number in numbers:
            dx, dy = LOWER[number]

            @pl.when(present(-dx, -dy))
            def _():
                pair_copy(number).wait_recv()

    carry_x[...] = jnp.zeros_like(carry_x)
    wait_halos((0,))
    pl.loop(1, size_x)(image_row)
    wait_halos((1,))
    image_row(0, lowest=True)
    totals = lax.fori_loop(0, size_y, node, (zero,) * 4, unroll=4)
    start_pair((0, 2))
    wait_halos((-1,))
    image_row(size_x)
    totals = lax.fori_loop(size_y, size_x * size_y, node, totals, unroll=4)
    start_pair((1,))

    for number, (dx, dy) in enumerate(LOWER):
        target_x, target_y = pair_edge(dx, size_x)[1], pair_edge(dy, size_y)[1]

        @pl.when(jnp.logical_not(present(-dx, -dy)))
        def _():
            shape = (6, target_x.size, target_y.size, rows, LANES)
            pair[:, target_x, target_y] = jnp.zeros(shape, jnp.float32)

    second_sums = sampled(pair, 0)

    def energy_row(x, energies):
        def body(y, carry):
            before, before_other, (first, mixed, last) = carry
            after = column_modes(pair, 0, x, y + 1)
            after_other = column_modes(pair, 3, x, y + 1)
            modes = element_modes(before, after)
            other = element_modes(before_other, after_other)
            scale = ext[6, x + 1, y + 1]
            forces, other_forces = apply_modes(modes), apply_modes(other)

            def dotted(left, right):
                total = None
                for key in TERMS:
                    term = left[key] * right[key]
                    total = term if total is None else total + term
                return total * scale

            first = first + dotted(modes, forces)
            mixed = mixed + dotted(other, forces)
            last = last + dotted(other, other_forces)
            return after, after_other, (first, mixed, last)

        start = (column_modes(pair, 0, x, 0), column_modes(pair, 3, x, 0), energies)
        return lax.fori_loop(0, size_y, body, start, unroll=UNROLL_ENERGY)[2]

    wait_pair((1,))
    energies = lax.fori_loop(0, size_x - 1, energy_row, (zero,) * 3)
    wait_pair((0, 2))
    energies = energy_row(size_x - 1, energies)

    payload = jnp.concatenate([first_sums, second_sums], axis=0)
    for number, total in enumerate(totals + energies):
        payload = jnp.where(lane == 64 + number, jnp.sum(total, axis=1, keepdims=True), payload)

    def summed(value, part, me, count, send, recv, device):
        part[me] = value
        for step in range(1, count):
            pltpu.make_async_remote_copy(
                src_ref=part.at[me],
                dst_ref=part.at[me],
                send_sem=send.at[step - 1],
                recv_sem=recv.at[step - 1],
                device_id=device(lax.rem(me + step, count)),
                device_id_type=MESH,
            ).start()
        for step in range(1, count):
            source = lax.rem(me - step + count, count)
            pltpu.make_async_remote_copy(
                src_ref=part.at[source],
                dst_ref=part.at[source],
                send_sem=send.at[step - 1],
                recv_sem=recv.at[step - 1],
                device_id=device(source),
                device_id_type=MESH,
            ).wait_recv()
        total = part[0]
        for index in range(1, count):
            total = total + part[index]
        return total

    total = summed(payload, slab_part, slab, slabs, slab_send, slab_recv, lambda i: (i, brick))
    total = summed(total, brick_part, brick, bricks, brick_send, brick_recv, lambda i: (slab, i))

    frame_one = iota((rows, LANES), 0) >= tiles

    def scalar(number):
        column = total[:, 64 + number : 65 + number]
        return (
            jnp.sum(column[:tiles], axis=0, keepdims=True),
            jnp.sum(column[tiles:], axis=0, keepdims=True),
        )

    sums = [scalar(number) for number in range(7)]
    factors = []
    for frame in range(FRAMES):
        norm, curve, cross, square, first, mixed, last = [pairs[frame] for pairs in sums]
        step = norm / curve
        norm_next = norm - 2.0 * step * cross + step * step * square
        ratio = norm_next / norm
        curve_next = (
            (first - 2.0 * step * mixed + step * step * last)
            + 2.0 * ratio * (cross - step * square)
            + ratio * ratio * curve
        )
        step_next = norm_next / curve_next
        factors.append((step + step_next * ratio, step_next, -step_next * step))
    wide = [jnp.where(frame_one, factors[1][i], factors[0][i]) for i in range(3)]

    for frame in range(FRAMES):
        line = total[frame : frame + 1]
        for i in range(3):
            at = 2 * (i + 1) + frame
            line = line + factors[frame][i] * total[at : at + 1]
        sens_ref[frame : frame + 1, :] = line[:, :MUSCLES]

    flat_image = image.reshape(6 * (size_x + 1) * (size_y + 1) * rows, LANES)

    @pl.loop(0, size_x * size_y, unroll=4)
    def _(column):
        x, y = column // size_y, column % size_y
        for c in range(3):
            image[c, x, y] = (
                ext[c, x + 1, y + 1]
                + wide[0] * ext[3 + c, x + 1, y + 1]
                + wide[1] * pair[c, x, y]
                + wide[2] * pair[3 + c, x, y]
            )

    for frame in range(FRAMES):
        for c in range(3):
            for x in range(size_x):
                for tile in range(tiles):
                    base = (c * (size_x + 1) + x) * (size_y + 1) * rows + frame * tiles + tile
                    out_ref[frame, c, x, :, tile * LANES : (tile + 1) * LANES] = flat_image[
                        pl.ds(base, size_y, stride=rows), :
                    ]

    for number, (dx, dy) in enumerate(DIRECTIONS):

        @pl.when(present(dx, dy))
        def _():
            halo(number).wait_send()

    for number, (dx, dy) in enumerate(LOWER):

        @pl.when(present(dx, dy))
        def _():
            pair_copy(number).wait_send()

    for part, me, count, send, recv, device in (
        (slab_part, slab, slabs, slab_send, slab_recv, lambda i: (i, brick)),
        (brick_part, brick, bricks, brick_send, brick_recv, lambda i: (slab, i)),
    ):
        for step in range(1, count):
            pltpu.make_async_remote_copy(
                src_ref=part.at[me],
                dst_ref=part.at[me],
                send_sem=send.at[step - 1],
                recv_sem=recv.at[step - 1],
                device_id=device(lax.rem(me + step, count)),
                device_id_type=MESH,
            ).wait_send()


def on_device(slabs, bricks, occupancy, modulus, start, direction, force, line, attachments):
    size_x, size_y, size_z = occupancy.shape
    tiles = size_z // LANES
    rows = FRAMES * tiles
    vmem = pl.BlockSpec(memory_space=pltpu.VMEM)
    dma = pltpu.SemaphoreType.DMA
    return pl.pallas_call(
        functools.partial(kernel, slabs, bricks),
        out_shape=(
            jax.ShapeDtypeStruct(start.shape, jnp.float32),
            jax.ShapeDtypeStruct(force.shape, jnp.float32),
        ),
        in_specs=[pl.BlockSpec(memory_space=pltpu.HBM)] * 7,
        out_specs=(vmem, vmem),
        scratch_shapes=[
            pltpu.VMEM(start.shape, jnp.float32),
            pltpu.VMEM(start.shape, jnp.float32),
            pltpu.VMEM(occupancy.shape, jnp.int32),
            pltpu.VMEM(occupancy.shape, jnp.float32),
            pltpu.VMEM((3, MUSCLES, ATTACH), jnp.int32),
            pltpu.VMEM((FRAMES, MUSCLES), jnp.float32),
            pltpu.VMEM((3, FRAMES, MUSCLES), jnp.float32),
            dma((7,)),
            pltpu.VMEM((7, size_x + 2, size_y + 2, rows, LANES), jnp.float32),
            pltpu.VMEM((6, size_x + 1, size_y + 1, rows, LANES), jnp.float32),
            pltpu.VMEM((6, size_y + 1, rows, LANES), jnp.float32),
            pltpu.VMEM((6, size_x + 1, size_y + 1, rows, LANES), jnp.float32),
            pltpu.VMEM((size_x * size_y, 3 * rows, LANES), jnp.float32),
            pltpu.VMEM((size_x * size_y, MUSCLES * tiles, LANES), jnp.float32),
            pltpu.VMEM((slabs, rows, LANES), jnp.float32),
            pltpu.VMEM((bricks, rows, LANES), jnp.float32),
            dma((8,)),
            dma((8,)),
            dma((3,)),
            dma((3,)),
            dma((slabs - 1,)),
            dma((slabs - 1,)),
            dma((bricks - 1,)),
            dma((bricks - 1,)),
        ],
        compiler_params=pltpu.CompilerParams(
            collective_id=0, has_side_effects=True, vmem_limit_bytes=60 * 1024 * 1024
        ),
    )(
        start,
        direction,
        occupancy,
        modulus,
        jnp.transpose(attachments, (2, 0, 1)),
        force,
        jnp.transpose(line, (2, 0, 1)),
    )


def solution(mesh):
    return jax.shard_map(
        functools.partial(on_device, mesh.shape["slab"], mesh.shape["brick"]),
        mesh=mesh,
        in_specs=(
            P("slab", "brick", None),
            P("slab", "brick", None),
            P(None, None, "slab", "brick", None),
            P(None, None, "slab", "brick", None),
            P(),
            P(),
            P(),
        ),
        out_specs=(P(None, None, "slab", "brick", None), P()),
        check_vma=False,
    )
```

```python
import functools
import math

import jax
import jax.numpy as jnp
import numpy as np
from jax import lax
from jax.experimental import pallas as pl
from jax.experimental.pallas import tpu as pltpu
from jax.sharding import PartitionSpec as P

MUSCLES = 40
ATTACH = 128
FRAMES = 2
LANES = 128
UNROLL_IMAGE = 3
UNROLL_ENERGY = 4

ersatz_modulus = 0.02
MESH = pl.DeviceIdType.MESH
HIGHEST = lax.Precision.HIGHEST
DIRECTIONS = [(dx, dy) for dx in (0, 1, -1) for dy in (0, 1, -1) if (dx, dy) != (0, 0)]
LOWER = [(-1, 0), (0, -1), (-1, -1)]


def corner_offsets():
    return [(step_x, step_y, step_z) for step_x in (0, 1) for step_y in (0, 1) for step_z in (0, 1)]


def element_matrix():
    poisson = 0.3
    lame_first = poisson / ((1.0 + poisson) * (1.0 - 2.0 * poisson))
    shear_modulus = 0.5 / (1.0 + poisson)
    elastic = np.zeros((6, 6))
    elastic[:3, :3] = lame_first
    for position in range(3):
        elastic[position, position] += 2.0 * shear_modulus
        elastic[position + 3, position + 3] = shear_modulus
    points = [0.5 - 0.5 / math.sqrt(3.0), 0.5 + 0.5 / math.sqrt(3.0)]
    matrix = np.zeros((24, 24))
    for point_x in points:
        for point_y in points:
            for point_z in points:
                strain = np.zeros((6, 24))
                for corner, (step_x, step_y, step_z) in enumerate(corner_offsets()):
                    weight_x = point_x if step_x else 1.0 - point_x
                    weight_y = point_y if step_y else 1.0 - point_y
                    weight_z = point_z if step_z else 1.0 - point_z
                    sign_x = 1.0 if step_x else -1.0
                    sign_y = 1.0 if step_y else -1.0
                    sign_z = 1.0 if step_z else -1.0
                    grad_x = sign_x * weight_y * weight_z
                    grad_y = weight_x * sign_y * weight_z
                    grad_z = weight_x * weight_y * sign_z
                    column = 3 * corner
                    strain[0, column] = grad_x
                    strain[1, column + 1] = grad_y
                    strain[2, column + 2] = grad_z
                    strain[3, column] = grad_y
                    strain[3, column + 1] = grad_x
                    strain[4, column + 1] = grad_z
                    strain[4, column + 2] = grad_y
                    strain[5, column] = grad_z
                    strain[5, column + 2] = grad_x
                matrix += strain.T @ elastic @ strain / 8.0
    return matrix


def mode_terms():
    corners = corner_offsets()
    signs = np.array(
        [
            [np.prod([1.0 if (not m or s) else -1.0 for m, s in zip(mode, step)]) for step in corners]
            for mode in corners
        ]
    )
    matrix = element_matrix().reshape(8, 3, 8, 3)
    modal = np.einsum("ma,aibj,nb->minj", signs, matrix, signs) / 64.0
    terms = {}
    for m, mode in enumerate(corners):
        for i in range(3):
            row = [
                ((j,) + corners[n], float(modal[m, i, n, j]))
                for n in range(8)
                for j in range(3)
                if abs(modal[m, i, n, j]) > 1e-9
            ]
            if row:
                terms[(i,) + mode] = row
    return terms


TERMS = mode_terms()
DIAGONAL = float(element_matrix()[0, 0])


def apply_modes(modes):
    forces = {}
    for key, row in TERMS.items():
        total = None
        for other, value in row:
            term = modes[other] * value
            total = term if total is None else total + term
        forces[key] = total
    return forces


def split_rows(values):
    high = values.astype(jnp.bfloat16)
    low = (values - high.astype(jnp.float32)).astype(jnp.bfloat16)
    return jnp.concatenate([high, low], axis=0)


def kernel(
    slabs,
    bricks,
    start_in,
    dir_in,
    occ_in,
    mod_in,
    att_in,
    force_in,
    line_in,
    out_ref,
    sens_ref,
    start_ref,
    dir_ref,
    occ_ref,
    mod_ref,
    att_ref,
    force_ref,
    line_ref,
    fetched,
    ext,
    image,
    carry_x,
    pair,
    load,
    counts,
    slab_part,
    brick_part,
    halo_send,
    halo_recv,
    pair_send,
    pair_recv,
    slab_send,
    slab_recv,
    brick_send,
    brick_recv,
):
    size_x, size_y, size_z = occ_ref.shape
    tiles = size_z // LANES
    rows = FRAMES * tiles
    slab = lax.axis_index("slab")
    brick = lax.axis_index("brick")
    barrier = pltpu.get_barrier_semaphore()
    sources = (start_in, dir_in, occ_in, mod_in, att_in, force_in, line_in)
    targets = (start_ref, dir_ref, occ_ref, mod_ref, att_ref, force_ref, line_ref)
    fetches = [
        pltpu.make_async_copy(source, target, fetched.at[number])
        for number, (source, target) in enumerate(zip(sources, targets))
    ]
    for fetch in fetches:
        fetch.start()

    def present(dx, dy):
        ok = None
        for delta, place, count in ((dx, slab, slabs), (dy, brick, bricks)):
            if delta == 0:
                continue
            here = (place > 0) if delta < 0 else (place < count - 1)
            ok = here if ok is None else ok & here
        return ok

    for step in range(1, slabs):
        pl.semaphore_signal(
            barrier, inc=1, device_id=(lax.rem(slab + step, slabs), brick), device_id_type=MESH
        )
    for step in range(1, bricks):
        pl.semaphore_signal(
            barrier, inc=1, device_id=(slab, lax.rem(brick + step, bricks)), device_id_type=MESH
        )
    for dx, dy in DIRECTIONS:
        if dx and dy:

            @pl.when(present(dx, dy))
            def _():
                pl.semaphore_signal(
                    barrier, inc=1, device_id=(slab + dx, brick + dy), device_id_type=MESH
                )

    flat = ext.reshape(7 * (size_x + 2) * (size_y + 2) * rows, LANES)
    zero = jnp.zeros((rows, LANES), jnp.float32)

    def place(field, x, row, value):
        base = ((field * (size_x + 2) + x + 1) * (size_y + 2) + 1) * rows + row
        flat[pl.ds(base, size_y, stride=rows), :] = value

    for fetch in fetches[:4]:
        fetch.wait()

    for x in range(size_x):
        for tile in range(tiles):
            part = slice(tile * LANES, (tile + 1) * LANES)
            bone = occ_ref[x, :, part].astype(jnp.float32)
            scale = bone * mod_ref[x, :, part] + (1.0 - bone) * ersatz_modulus
            for frame in range(FRAMES):
                row = frame * tiles + tile
                place(6, x, row, scale)
                for c in range(3):
                    place(c, x, row, start_ref[frame, c, x, :, part])
                    place(3 + c, x, row, dir_ref[frame, c, x, :, part])

    def edge(delta, size):
        if delta == 0:
            return pl.ds(1, size), pl.ds(1, size)
        return (pl.ds(1, 1), pl.ds(size + 1, 1)) if delta < 0 else (pl.ds(size, 1), pl.ds(0, 1))

    def halo(number):
        dx, dy = DIRECTIONS[number]
        source_x, target_x = edge(dx, size_x)
        source_y, target_y = edge(dy, size_y)
        fields = pl.ds(0, 7 if dx >= 0 and dy >= 0 else 6)
        return pltpu.make_async_remote_copy(
            src_ref=ext.at[fields, source_x, source_y],
            dst_ref=ext.at[fields, target_x, target_y],
            send_sem=halo_send.at[number],
            recv_sem=halo_recv.at[number],
            device_id=(slab + dx, brick + dy),
            device_id_type=MESH,
        )

    for number, (dx, dy) in enumerate(DIRECTIONS):
        back_x, back_y = edge(dx, size_x)[1], edge(dy, size_y)[1]

        @pl.when(jnp.logical_not(present(-dx, -dy)))
        def _():
            shape = (7, back_x.size, back_y.size, rows, LANES)
            ext[:, back_x, back_y] = jnp.zeros(shape, jnp.float32)

    amount = slabs + bricks - 2
    for dx, dy in DIRECTIONS:
        if dx and dy:
            amount = amount + present(dx, dy).astype(jnp.int32)
    pl.semaphore_wait(barrier, amount)

    for number, (dx, dy) in enumerate(DIRECTIONS):

        @pl.when(present(dx, dy))
        def _():
            halo(number).start()

    width = 2 * ATTACH
    span = MUSCLES * tiles
    row_ids = lax.broadcasted_iota(jnp.int32, (size_x * size_y * 2 * tiles, width), 0)
    lane_ids = lax.broadcasted_iota(jnp.int32, (LANES, width), 0)
    second = (lax.broadcasted_iota(jnp.int32, (1, width), 1) >= ATTACH).astype(jnp.int32)

    for fetch in fetches[4:]:
        fetch.wait()

    @pl.loop(0, MUSCLES // 2, unroll=10)
    def _(two):
        def both(dim):
            return jnp.concatenate(
                [att_ref[dim, pl.ds(2 * two, 1), :], att_ref[dim, pl.ds(2 * two + 1, 1), :]], axis=1
            )

        near_x = both(0) - slab * size_x
        near_y = both(1) - brick * size_y
        far = both(2)
        tile = lax.shift_right_logical(far, 7)
        inside = (near_x >= 0) & (near_x < size_x) & (near_y >= 0) & (near_y < size_y)
        code = ((near_x * size_y + near_y) * 2 + second) * tiles + tile
        code = jnp.where(inside, code, -1)
        hits = jnp.where(row_ids == code, 1.0, 0.0).astype(jnp.bfloat16)
        depth = jnp.where(lane_ids == far - tile * LANES, 1.0, 0.0).astype(jnp.bfloat16)
        found = lax.dot_general(
            hits, depth, (((1,), (1,)), ((), ())), preferred_element_type=jnp.float32
        )
        counts[:, pl.ds(pl.multiple_of(two * 2 * tiles, 8), 2 * tiles), :] = found.reshape(
            size_x * size_y, 2 * tiles, LANES
        )

    def iota(shape, dim):
        return lax.broadcasted_iota(jnp.int32, shape, dim)

    def dot32(left, right):
        return jnp.dot(left, right, precision=HIGHEST, preferred_element_type=jnp.float32)

    def ones_where(mask):
        return jnp.where(mask, 1.0, 0.0)

    spread_rows = ones_where(iota((24, 6), 0) // tiles == iota((24, 6), 1))
    spread_cols = ones_where(iota((MUSCLES, span), 1) // tiles == iota((MUSCLES, span), 0))
    same_tile = ones_where(iota((24, span), 0) % tiles == iota((24, span), 1) % tiles)
    lines = jnp.concatenate([line_ref[c] for c in range(3)], axis=0) * (1.0 / ATTACH)
    forces = jnp.concatenate([force_ref[...]] * 3, axis=0)
    line_wide = dot32(spread_rows, dot32(lines, spread_cols)) * same_tile
    load_wide = split_rows(dot32(spread_rows, dot32(lines * forces, spread_cols)) * same_tile)

    @pl.loop(0, size_x * size_y, unroll=16)
    def _(column):
        both = jnp.dot(
            load_wide, counts[column].astype(jnp.bfloat16), preferred_element_type=jnp.float32
        )
        load[column] = both[:24] + both[24:]

    def sampled(ref, offset):
        def body(column, total):
            x, y = column // size_y, column % size_y
            values = ref[pl.ds(0, 6), x + offset, y + offset].reshape(6 * rows, LANES)
            return total + lax.dot_general(
                split_rows(values),
                counts[column].astype(jnp.bfloat16),
                (((1,), (1,)), ((), ())),
                preferred_element_type=jnp.float32,
            )

        both = lax.fori_loop(
            0, size_x * size_y, body, jnp.zeros((12 * rows, span), jnp.float32), unroll=16
        )
        total = (both[: 6 * rows] + both[6 * rows :]) * jnp.concatenate([line_wide] * 2, axis=0)
        shape = (4, 6 * rows)
        at = iota(shape, 1)
        pick = (at // 24 == iota(shape, 0) // 2) & ((at // tiles) % 2 == iota(shape, 0) % 2)
        narrow = ones_where(iota((span, LANES), 0) // tiles == iota((span, LANES), 1))
        return dot32(dot32(ones_where(pick), total), narrow)

    first_sums = sampled(ext, 1)

    lane = iota((rows, LANES), 1)
    tile_of = iota((rows, LANES), 0) % tiles
    is_last, is_first = lane == LANES - 1, lane == 0
    keep_up = ones_where(tile_of != tiles - 1)
    keep_down = ones_where(tile_of != 0)

    def from_above(value):
        turned = pltpu.roll(value, LANES - 1, 1)
        return jnp.where(is_last, pltpu.roll(turned, rows - 1, 0) * keep_up, turned)

    def from_below(value):
        turned = pltpu.roll(value, 1, 1)
        return jnp.where(is_first, pltpu.roll(turned, 1, 0) * keep_down, turned)

    def column_modes(ref, field, x, y):
        found = []
        for c in range(3):
            low, high = ref[field + c, x, y], ref[field + c, x + 1, y]
            for value in (high + low, high - low):
                above = from_above(value)
                found += [above + value, above - value]
        return tuple(found)

    def element_modes(before, after):
        modes = {}
        for c in range(3):
            for mx in (0, 1):
                for mz in (0, 1):
                    low, high = before[c * 4 + mx * 2 + mz], after[c * 4 + mx * 2 + mz]
                    modes[c, mx, 0, mz] = high + low
                    modes[c, mx, 1, mz] = high - low
        return modes

    def wait_halos(wanted):
        for number, (dx, dy) in enumerate(DIRECTIONS):
            if dx in wanted:

                @pl.when(present(-dx, -dy))
                def _():
                    halo(number).wait_recv()

    def image_row(x, lowest=False):
        def body(y, carry):
            after_both, later_both = [], []
            scale = ext[6, x, y]
            for half in (0, 1):
                before, pending = carry[0][half], carry[1][half]
                after = column_modes(ext, 3 * half, x, y + 1)
                forces = apply_modes(element_modes(before, after))
                later = []
                for c in range(3):
                    parts = []
                    for mx in (0, 1):
                        done = []
                        for mz in (0, 1):
                            odd = forces[c, mx, 1, mz] * scale
                            if (c, mx, 0, mz) in forces:
                                even = forces[c, mx, 0, mz] * scale
                                low, high = even - odd, even + odd
                            else:
                                low, high = -odd, odd
                            done.append(low + pending[c * 4 + mx * 2 + mz])
                            later.append(high)
                        parts.append((done[0] - done[1]) + from_below(done[0] + done[1]))
                    index = 3 * half + c
                    if lowest:
                        image[index, 1, y] += parts[0] + parts[1]
                    else:
                        image[index, x, y] = carry_x[index, y] + (parts[0] - parts[1])
                        carry_x[index, y] = parts[0] + parts[1]
                after_both.append(after)
                later_both.append(tuple(later))
            return tuple(after_both), tuple(later_both)

        first = tuple(column_modes(ext, 3 * half, x, 0) for half in (0, 1))
        lax.fori_loop(0, size_y + 1, body, (first, ((zero,) * 12,) * 2), unroll=UNROLL_IMAGE)

    def node(column, totals):
        x, y = column // size_y, column % size_y
        around = (ext[6, x, y] + ext[6, x, y + 1]) + (ext[6, x + 1, y] + ext[6, x + 1, y + 1])
        inverse = 1.0 / ((around + from_below(around)) * DIAGONAL)
        norm, curve, cross, square = totals
        for c in range(3):
            residual = load[column, pl.ds(c * rows, rows), :] - image[c, x + 1, y + 1]
            stiff = image[3 + c, x + 1, y + 1]
            scaled, other = residual * inverse, stiff * inverse
            pair[c, x, y] = scaled
            pair[3 + c, x, y] = other
            norm = norm + residual * scaled
            curve = curve + ext[3 + c, x + 1, y + 1] * stiff
            cross = cross + residual * other
            square = square + stiff * other
        return norm, curve, cross, square

    def pair_edge(delta, size):
        return (pl.ds(0, size), pl.ds(0, size)) if delta == 0 else (pl.ds(0, 1), pl.ds(size, 1))

    def pair_copy(number):
        dx, dy = LOWER[number]
        source_x, target_x = pair_edge(dx, size_x)
        source_y, target_y = pair_edge(dy, size_y)
        return pltpu.make_async_remote_copy(
            src_ref=pair.at[:, source_x, source_y],
            dst_ref=pair.at[:, target_x, target_y],
            send_sem=pair_send.at[number],
            recv_sem=pair_recv.at[number],
            device_id=(slab + dx, brick + dy),
            device_id_type=MESH,
        )

    def start_pair(numbers):
        for number in numbers:

            @pl.when(present(*LOWER[number]))
            def _():
                pair_copy(number).start()

    def wait_pair(numbers):
        for number in numbers:
            dx, dy = LOWER[number]

            @pl.when(present(-dx, -dy))
            def _():
                pair_copy(number).wait_recv()

    carry_x[...] = jnp.zeros_like(carry_x)
    wait_halos((0,))
    pl.loop(1, size_x)(image_row)
    wait_halos((1,))
    image_row(0, lowest=True)
    totals = lax.fori_loop(0, size_y, node, (zero,) * 4, unroll=8)
    start_pair((0, 2))
    wait_halos((-1,))
    image_row(size_x)
    totals = lax.fori_loop(size_y, size_x * size_y, node, totals, unroll=8)
    start_pair((1,))

    for number, (dx, dy) in enumerate(LOWER):
        target_x, target_y = pair_edge(dx, size_x)[1], pair_edge(dy, size_y)[1]

        @pl.when(jnp.logical_not(present(-dx, -dy)))
        def _():
            shape = (6, target_x.size, target_y.size, rows, LANES)
            pair[:, target_x, target_y] = jnp.zeros(shape, jnp.float32)

    second_sums = sampled(pair, 0)

    def energy_row(x, energies):
        def body(y, carry):
            before, before_other, (first, mixed, last) = carry
            after = column_modes(pair, 0, x, y + 1)
            after_other = column_modes(pair, 3, x, y + 1)
            modes = element_modes(before, after)
            other = element_modes(before_other, after_other)
            scale = ext[6, x + 1, y + 1]
            forces, other_forces = apply_modes(modes), apply_modes(other)

            def dotted(left, right):
                total = None
                for key in TERMS:
                    term = left[key] * right[key]
                    total = term if total is None else total + term
                return total * scale

            first = first + dotted(modes, forces)
            mixed = mixed + dotted(other, forces)
            last = last + dotted(other, other_forces)
            return after, after_other, (first, mixed, last)

        start = (column_modes(pair, 0, x, 0), column_modes(pair, 3, x, 0), energies)
        return lax.fori_loop(0, size_y, body, start, unroll=UNROLL_ENERGY)[2]

    wait_pair((1,))
    energies = lax.fori_loop(0, size_x - 1, energy_row, (zero,) * 3)
    wait_pair((0, 2))
    energies = energy_row(size_x - 1, energies)

    payload = jnp.concatenate([first_sums, second_sums], axis=0)
    for number, total in enumerate(totals + energies):
        payload = jnp.where(lane == 64 + number, jnp.sum(total, axis=1, keepdims=True), payload)

    def summed(value, part, me, count, send, recv, device):
        part[me] = value
        for step in range(1, count):
            pltpu.make_async_remote_copy(
                src_ref=part.at[me],
                dst_ref=part.at[me],
                send_sem=send.at[step - 1],
                recv_sem=recv.at[step - 1],
                device_id=device(lax.rem(me + step, count)),
                device_id_type=MESH,
            ).start()
        for step in range(1, count):
            source = lax.rem(me - step + count, count)
            pltpu.make_async_remote_copy(
                src_ref=part.at[source],
                dst_ref=part.at[source],
                send_sem=send.at[step - 1],
                recv_sem=recv.at[step - 1],
                device_id=device(source),
                device_id_type=MESH,
            ).wait_recv()
        total = part[0]
        for index in range(1, count):
            total = total + part[index]
        return total

    total = summed(payload, slab_part, slab, slabs, slab_send, slab_recv, lambda i: (i, brick))
    total = summed(total, brick_part, brick, bricks, brick_send, brick_recv, lambda i: (slab, i))

    frame_one = iota((rows, LANES), 0) >= tiles

    def scalar(number):
        column = total[:, 64 + number : 65 + number]
        return (
            jnp.sum(column[:tiles], axis=0, keepdims=True),
            jnp.sum(column[tiles:], axis=0, keepdims=True),
        )

    sums = [scalar(number) for number in range(7)]
    factors = []
    for frame in range(FRAMES):
        norm, curve, cross, square, first, mixed, last = [pairs[frame] for pairs in sums]
        step = norm / curve
        norm_next = norm - 2.0 * step * cross + step * step * square
        ratio = norm_next / norm
        curve_next = (
            (first - 2.0 * step * mixed + step * step * last)
            + 2.0 * ratio * (cross - step * square)
            + ratio * ratio * curve
        )
        step_next = norm_next / curve_next
        factors.append((step + step_next * ratio, step_next, -step_next * step))
    wide = [jnp.where(frame_one, factors[1][i], factors[0][i]) for i in range(3)]

    for frame in range(FRAMES):
        line = total[frame : frame + 1]
        for i in range(3):
            at = 2 * (i + 1) + frame
            line = line + factors[frame][i] * total[at : at + 1]
        sens_ref[frame : frame + 1, :] = line[:, :MUSCLES]

    flat_image = image.reshape(6 * (size_x + 1) * (size_y + 1) * rows, LANES)

    @pl.loop(0, size_x * size_y, unroll=8)
    def _(column):
        x, y = column // size_y, column % size_y
        for c in range(3):
            image[c, x, y] = (
                ext[c, x + 1, y + 1]
                + wide[0] * ext[3 + c, x + 1, y + 1]
                + wide[1] * pair[c, x, y]
                + wide[2] * pair[3 + c, x, y]
            )

    for frame in range(FRAMES):
        for c in range(3):
            for x in range(size_x):
                for tile in range(tiles):
                    base = (c * (size_x + 1) + x) * (size_y + 1) * rows + frame * tiles + tile
                    out_ref[frame, c, x, :, tile * LANES : (tile + 1) * LANES] = flat_image[
                        pl.ds(base, size_y, stride=rows), :
                    ]

    for number, (dx, dy) in enumerate(DIRECTIONS):

        @pl.when(present(dx, dy))
        def _():
            halo(number).wait_send()

    for number, (dx, dy) in enumerate(LOWER):

        @pl.when(present(dx, dy))
        def _():
            pair_copy(number).wait_send()

    for part, me, count, send, recv, device in (
        (slab_part, slab, slabs, slab_send, slab_recv, lambda i: (i, brick)),
        (brick_part, brick, bricks, brick_send, brick_recv, lambda i: (slab, i)),
    ):
        for step in range(1, count):
            pltpu.make_async_remote_copy(
                src_ref=part.at[me],
                dst_ref=part.at[me],
                send_sem=send.at[step - 1],
                recv_sem=recv.at[step - 1],
                device_id=device(lax.rem(me + step, count)),
                device_id_type=MESH,
            ).wait_send()


def on_device(slabs, bricks, occupancy, modulus, start, direction, force, line, attachments):
    size_x, size_y, size_z = occupancy.shape
    tiles = size_z // LANES
    rows = FRAMES * tiles
    vmem = pl.BlockSpec(memory_space=pltpu.VMEM)
    dma = pltpu.SemaphoreType.DMA
    return pl.pallas_call(
        functools.partial(kernel, slabs, bricks),
        out_shape=(
            jax.ShapeDtypeStruct(start.shape, jnp.float32),
            jax.ShapeDtypeStruct(force.shape, jnp.float32),
        ),
        in_specs=[pl.BlockSpec(memory_space=pltpu.HBM)] * 7,
        out_specs=(vmem, vmem),
        scratch_shapes=[
            pltpu.VMEM(start.shape, jnp.float32),
            pltpu.VMEM(start.shape, jnp.float32),
            pltpu.VMEM(occupancy.shape, jnp.int32),
            pltpu.VMEM(occupancy.shape, jnp.float32),
            pltpu.VMEM((3, MUSCLES, ATTACH), jnp.int32),
            pltpu.VMEM((FRAMES, MUSCLES), jnp.float32),
            pltpu.VMEM((3, FRAMES, MUSCLES), jnp.float32),
            dma((7,)),
            pltpu.VMEM((7, size_x + 2, size_y + 2, rows, LANES), jnp.float32),
            pltpu.VMEM((6, size_x + 1, size_y + 1, rows, LANES), jnp.float32),
            pltpu.VMEM((6, size_y + 1, rows, LANES), jnp.float32),
            pltpu.VMEM((6, size_x + 1, size_y + 1, rows, LANES), jnp.float32),
            pltpu.VMEM((size_x * size_y, 3 * rows, LANES), jnp.float32),
            pltpu.VMEM((size_x * size_y, MUSCLES * tiles, LANES), jnp.float32),
            pltpu.VMEM((slabs, rows, LANES), jnp.float32),
            pltpu.VMEM((bricks, rows, LANES), jnp.float32),
            dma((8,)),
            dma((8,)),
            dma((3,)),
            dma((3,)),
            dma((slabs - 1,)),
            dma((slabs - 1,)),
            dma((bricks - 1,)),
            dma((bricks - 1,)),
        ],
        compiler_params=pltpu.CompilerParams(
            collective_id=0, has_side_effects=True, vmem_limit_bytes=60 * 1024 * 1024
        ),
    )(
        start,
        direction,
        occupancy,
        modulus,
        jnp.transpose(attachments, (2, 0, 1)),
        force,
        jnp.transpose(line, (2, 0, 1)),
    )


def solution(mesh):
    return jax.shard_map(
        functools.partial(on_device, mesh.shape["slab"], mesh.shape["brick"]),
        mesh=mesh,
        in_specs=(
            P("slab", "brick", None),
            P("slab", "brick", None),
            P(None, None, "slab", "brick", None),
            P(None, None, "slab", "brick", None),
            P(),
            P(),
            P(),
        ),
        out_specs=(P(None, None, "slab", "brick", None), P()),
        check_vma=False,
    )
```
